512 devices in a mesh: blk: 32 (over z_lo, x), pen: 16 (over z_hi, y, core).
Axes of the slice: x: 4, y: 4, z: 16 (z_hi: 2, z_lo: 8; z = z_hi * 8 + z_lo), core: 2. Of those that a mesh axis runs over, the one named last changes fastest.
Arguments:
- state: float32 [32, 128, 5, 1024], P('blk', 'pen'), may hold values from -6 to 6
- previous: float32 [32, 128, 5, 1024], P('blk', 'pen'), may hold values from -6 to 6
- iblank: int32 [32, 128, 1024], P('blk', 'pen'), may hold values 0 or 1
- block_owner: int32 [32], replicated, may hold values from 0 to 31, as said below
- donor_cell: int32 [16, 32, 32, 128, 8], P('pen', 'blk'), may hold values from 0 to 8191
- donor_weight: float32 [16, 32, 32, 128, 8], P('pen', 'blk'), may hold values from 0.02 to 0.25
- send_count: int32 [16, 32, 32], P('pen', 'blk'), may hold values from 0 to 128, as said below
- recv_cell: int32 [16, 32, 32, 128], P('pen', 'blk'), may hold values from 0 to 8191, as said below
- speed: float32 [32, 5, 1024], P('blk'), may hold values from -1 to 1
- left_vectors: float32 [32, 5, 5, 1024], P('blk'), may hold values from -2.5 to 2.5
- right_vectors: float32 [32, 5, 5, 1024], P('blk'), may hold values from -2.5 to 2.5
- line_inverse: float32 [32, 5, 128, 128], P('blk')
Outputs:
- updated: float32 [32, 128, 5, 1024], P('blk', 'pen')
The draws below stay inside these ranges and needn't reach their ends.
Inputs may be any that keep to these rules, and one draw needn't show every extreme that they name: `block_owner`: each device holds exactly one block. `donor_cell`: donor cells lie among the slab's first min(8192, 16368) cells. Slots at or past the live count hold valid cell numbers that are not used. `send_count`: A device sends no rows to its own block. At most 128 rows go from one device to one block; in every draw each device sends exactly 128 rows to some block of each slab. `recv_cell`: for one device and slab, the cells of all slots over all sending blocks are distinct.
All inputs are finite; a program needn't handle non-finite values. No bound on the sum of `iblank` on one device may be relied on, other than what follows from the above.
Results may differ from the reference program's by a relative error of at most 0.0001.
Values sent between devices are 32-bit elements; how exact they have to be, the bound alone decides.
A program may use at most 192 MiB of HBM per device.

```python
import jax
import jax.numpy as jnp
from jax import lax

NF = 5
ND = 8
J = 128
P_SIZE = 1024
NB = 32
CAP = 128
N_PEN = 16


def shared_owner(key):
    return jax.random.permutation(jax.random.fold_in(key, 11), NB).astype(jnp.int32)


def draw_block_owner(key, part):
    owner = shared_owner(key)
    return owner.astype(jnp.int32)


def draw_send_count(key, part):
    owner = shared_owner(key)
    key = jax.random.fold_in(key, 3)
    key_near, key_rest = jax.random.split(key, 2)
    device = jnp.arange(NB, dtype=jnp.int32)[None, :, None]
    offset = (device - owner[None, None, :]) % NB
    near = jax.random.randint(key_near, (N_PEN, NB, NB), CAP // 4, CAP + 1)
    rest = jax.random.randint(key_rest, (N_PEN, NB, NB), CAP // 8, 3 * CAP // 4 + 1)
    is_near = (offset == 1) | (offset == NB - 1)
    counts = jnp.where(is_near, near, rest)
    counts = jnp.where(offset == NB // 2, CAP, counts)
    counts = jnp.where(offset == 0, 0, counts)
    return counts.astype(jnp.int32)


def draw_recv_cell(key, part):
    key = jax.random.fold_in(key, 5)
    keys = jax.random.split(key, N_PEN * NB)
    ncells = J // N_PEN * P_SIZE
    perms = jax.vmap(lambda single: jax.random.permutation(single, ncells))(keys)
    perms = perms[:, :NB * CAP]
    return perms.reshape(N_PEN, NB, NB, CAP).astype(jnp.int32)


def draw_line_inverse(key, part):
    key = jax.random.fold_in(key, 7)
    key_len, key_rough = jax.random.split(key)
    lengths = jnp.exp(jax.random.uniform(key_len, (NB, NF, 1, 1), jnp.float32, jnp.log(24.0), jnp.log(192.0)))
    rough = jax.random.uniform(key_rough, (NB, NF, J, J), jnp.float32, 0.5, 1.5)
    points = jnp.arange(J, dtype=jnp.float32)
    gap = jnp.abs(points[:, None] - points[None, :])
    decay = jnp.exp(-gap[None, None] / lengths)
    return (jnp.eye(J, dtype=jnp.float32)[None, None] + decay * rough * (8.0 / lengths)).astype(jnp.float32)


def place_ends(array, key, smallest, top_value):
    longest = array.shape.index(max(array.shape))
    spots = []
    for shift in (0, 1):
        where = [jax.random.randint(jax.random.fold_in(key, axis), (), 0, length) for axis, length in enumerate(array.shape)]
        where[longest] = (where[longest] + shift) % array.shape[longest]
        spots.append(tuple(where))
    return array.at[spots[0]].set(smallest).at[spots[1]].set(top_value)


def block_scale(own_key, shape, cuts, low, top_value):
    loudness, own = 1.0, jax.random.fold_in(own_key, 6)
    for position, blocks in cuts:
        heights = jnp.exp(jax.random.uniform(jax.random.fold_in(own, position), (blocks,), jnp.float32, low / len(cuts), top_value / len(cuts)))
        loudness = loudness * jnp.repeat(heights, shape[position] // blocks).reshape([-1 if axis == position else 1 for axis in range(len(shape))])
    return loudness


def centred(key, extent, deviation, reach, cuts=(), kind=jnp.bfloat16):
    values = deviation * jax.random.normal(key, extent, jnp.float32)
    if cuts:
        values = values * block_scale(key, extent, cuts, -0.22, 0.18)
    return jnp.clip(values, -reach, reach).astype(kind)


def setup_inputs(seed: int = 0) -> dict:
    seeds = jax.random.split(jax.random.key(seed), 13)
    state = centred(seeds[0], (NB, J, NF, P_SIZE), 1.0, 6.0, ((0, 32), (1, 16)), jnp.float32)
    previous = centred(seeds[1], (NB, J, NF, P_SIZE), 1.0, 6.0, ((0, 32), (1, 16)), jnp.float32)
    iblank = place_ends((jax.random.randint(seeds[2], (NB, J, P_SIZE), 0, 8) < 7).astype(jnp.int32), jax.random.fold_in(seeds[2], 1), 0, 1)
    block_owner = draw_block_owner(jax.random.fold_in(seeds[12], 71), 0)
    donor_cell = place_ends(jax.random.randint(seeds[4], (N_PEN, NB, NB, CAP, ND), 0, min(J // N_PEN * P_SIZE, 16368)), jax.random.fold_in(seeds[4], 1), 0, (min(J // N_PEN * P_SIZE, 16368)) - 1).astype(jnp.int32)
    donor_weight = jnp.clip(0.02 + 0.23 * jax.random.uniform(seeds[5], (N_PEN, NB, NB, CAP, ND), jnp.float32) ** block_scale(seeds[5], (N_PEN, NB, NB, CAP, ND), ((0, 16), (1, 32)), -0.2, 0.2), 0.02, 0.25)
    send_count = draw_send_count(jax.random.fold_in(seeds[12], 71), 0)
    recv_cell = draw_recv_cell(jax.random.fold_in(seeds[12], 71), 0)
    speed = jnp.clip(jax.random.uniform(seeds[8], (NB, NF, P_SIZE), jnp.float32, -1.0, 1.0) * block_scale(seeds[8], (NB, NF, P_SIZE), ((0, 32),), -0.4, 0.0), -1.0, 1.0)
    left_vectors = centred(seeds[9], (NB, NF, NF, P_SIZE), NF ** -0.5, 2.5, ((0, 32),), jnp.float32)
    right_vectors = centred(seeds[10], (NB, NF, NF, P_SIZE), NF ** -0.5, 2.5, ((0, 32),), jnp.float32)
    line_inverse = draw_line_inverse(jax.random.fold_in(seeds[12], 71), 0)
    return dict(state=state, previous=previous, iblank=iblank, block_owner=block_owner, donor_cell=donor_cell, donor_weight=donor_weight, send_count=send_count, recv_cell=recv_cell, speed=speed, left_vectors=left_vectors, right_vectors=right_vectors, line_inverse=line_inverse)


def slab_fringe(slab, owner, held, cells, weights, counts, receivers):
    nblocks, depth, nfields, pencils = slab.shape
    ncells = depth * pencils
    flat = slab.transpose(0, 2, 1, 3).reshape(nblocks, nfields, ncells)

    def interpolate(args):
        values, index, weight = args
        picked = values[:, index]
        return jnp.sum(picked * weight[None], axis=-1)

    rows = lax.map(interpolate, (flat, cells, weights))
    arrived = rows[owner][:, :, held]
    arrived = arrived.transpose(2, 1, 0, 3)
    live_counts = counts[owner][:, held].transpose(1, 0)
    slots = jnp.arange(receivers.shape[-1], dtype=jnp.int32)
    live = slots[None, None, :] < live_counts[:, :, None]
    target = jnp.where(live, receivers, ncells).astype(jnp.int32)

    def place(values, index, incoming):
        return values.at[:, index.reshape(-1)].set(incoming.reshape(nfields, -1), mode="drop")

    flat = jax.vmap(place)(flat, target, arrived)
    return flat.reshape(nblocks, nfields, depth, pencils).transpose(0, 2, 1, 3)


def reference(state, previous, iblank, block_owner, donor_cell, donor_weight, send_count, recv_cell, speed, left_vectors, right_vectors, line_inverse):
    depth = J // N_PEN
    blocks = jnp.arange(NB, dtype=jnp.int32)
    match = block_owner[:, None] == blocks[None, :]
    held = jnp.sum(jnp.where(match, blocks[:, None], 0), axis=0).astype(jnp.int32)
    pieces = []
    for slab_index in range(N_PEN):
        slab = state[:, slab_index * depth:(slab_index + 1) * depth]
        pieces.append(slab_fringe(slab, block_owner, held, donor_cell[slab_index], donor_weight[slab_index], send_count[slab_index], recv_cell[slab_index]))
    filled = jnp.concatenate(pieces, axis=1)
    padded = jnp.pad(filled, ((0, 0), (2, 2), (0, 0), (0, 0)))
    upper = padded[:, 3:-1]
    lower = padded[:, 1:-3]
    upper_two = padded[:, 4:]
    lower_two = padded[:, :-4]
    wave = speed[:, None]
    resid = -(filled - previous) - 0.5 * wave * (upper - lower)
    resid = resid + 0.25 * (upper - 2.0 * filled + lower)
    resid = resid - 0.0625 * (upper_two - 4.0 * upper + 6.0 * filled - 4.0 * lower + lower_two)
    resid = resid - 0.25 * (jnp.roll(filled, -1, axis=-1) - jnp.roll(filled, 1, axis=-1))
    keep = iblank.astype(jnp.float32)[:, :, None, :]
    resid = resid * keep
    high = lax.Precision.HIGHEST
    work = jnp.einsum("bmnp,bjnp->bjmp", left_vectors, resid, precision=high)
    solved = jnp.einsum("bmjk,bkmp->bjmp", line_inverse, work, precision=high)
    change = jnp.einsum("bmnp,bjnp->bjmp", right_vectors, solved, precision=high)
    return filled + keep * change
```

```python
import functools

import jax
import jax.numpy as jnp
from jax import lax
from jax.experimental import pallas as pl
from jax.experimental.pallas import tpu as pltpu
from jax.sharding import PartitionSpec as P

MESH = pl.DeviceIdType.MESH
LANES = 128
DEAD = 1e30
TOGETHER = 4
INVERTED = 4


def lane_pick(table, index):
    return jnp.take_along_axis(table, index, axis=1, mode="promise_in_bounds")


def log2(n):
    assert n & (n - 1) == 0
    return n.bit_length() - 1


def kernel(
    n_blk,
    n_pen,
    owner_hbm,
    count_hbm,
    state_hbm,
    prev_hbm,
    iblank_hbm,
    dcell_hbm,
    dweight_hbm,
    rcell_hbm,
    speed_hbm,
    left_hbm,
    right_hbm,
    linv_hbm,
    out_ref,
    owner_ref,
    count_ref,
    state_ref,
    prev_ref,
    iblank_ref,
    dcell_ref,
    dweight_ref,
    rcell_ref,
    speed_ref,
    left_ref,
    right_ref,
    linv_ref,
    load_sem,
    held_vec,
    held_ref,
    held_sem,
    inv_ref,
    rows_out,
    rows_in,
    filled,
    halo_out,
    halo_in,
    resid,
    work,
    parts_in,
    work_line,
    solved_line,
    solved,
    fringe_send,
    fringe_recv,
    halo_send,
    halo_recv,
    fwd_send,
    fwd_recv,
    back_send,
    back_recv,
):
    nf, depth, pencils = state_hbm.shape
    groups = pencils // LANES
    n_a = n_pen // 2
    assert n_a == groups and depth == 8 and nf == 5
    n_hi = groups * depth
    p_bits, g_bits = log2(pencils), log2(groups)
    f32, i32 = jnp.float32, jnp.int32

    me_b = lax.axis_index("blk")
    me_p = lax.axis_index("pen")
    zh = lax.div(me_p, n_a)
    a = lax.rem(me_p, n_a)
    third = lax.rem(a, 2) == zh

    def lane_group(g):
        return pl.ds(pl.multiple_of(g * LANES, LANES), LANES)

    @pl.when(me_p == 0)
    def _():
        halo_in[0] = jnp.zeros(halo_in.shape[1:], f32)

    @pl.when(me_p == n_pen - 1)
    def _():
        halo_in[1] = jnp.zeros(halo_in.shape[1:], f32)

    barrier = pltpu.get_barrier_semaphore()

    def greet_blk(off, _):
        pl.semaphore_signal(barrier, inc=1, device_id={"blk": lax.rem(me_b + off, n_blk)}, device_id_type=MESH)
        return 0

    def greet_pen(off, _):
        pl.semaphore_signal(barrier, inc=1, device_id={"pen": lax.rem(me_p + off, n_pen)}, device_id_type=MESH)
        return 0

    lax.fori_loop(1, n_blk, greet_blk, 0)
    lax.fori_loop(1, n_pen, greet_pen, 0)

    loads = {}
    for name, source, target in (
        ("rcell", rcell_hbm, rcell_ref),
        ("owner", owner_hbm, owner_ref),
        ("count", count_hbm, count_ref),
        ("state", state_hbm, state_ref),
        ("dcell", dcell_hbm, dcell_ref),
        ("dweight", dweight_hbm, dweight_ref),
        ("prev", prev_hbm, prev_ref),
        ("iblank", iblank_hbm, iblank_ref),
        ("speed", speed_hbm, speed_ref),
        ("left", left_hbm, left_ref),
        ("linv", linv_hbm, linv_ref),
        ("right", right_hbm, right_ref),
    ):
        loads[name] = pltpu.make_async_copy(source, target, load_sem.at[len(loads)])
        loads[name].start()

    def loaded(*names):
        for name in names:
            loads[name].wait()

    lane = lax.broadcasted_iota(i32, (1, LANES), 1)
    hi_iota = lax.broadcasted_iota(i32, (n_hi, LANES), 0)
    lo_iota = lax.broadcasted_iota(i32, (LANES, LANES), 0)

    def invert(step, acc):
        tall, flat = [], []
        for u in range(INVERTED):
            b = step * INVERTED + u
            c = rcell_ref[pl.ds(b, 1), :]
            j = lax.shift_right_logical(c, p_bits)
            g = lax.shift_right_logical(c, 7) & (groups - 1)
            at_hi = hi_iota == g * depth + j
            slot = jnp.where(at_hi, (lane + 1).astype(f32), 0.0)
            block = jnp.where(at_hi, (b + 1).astype(f32), 0.0)
            tall.append(jnp.concatenate([slot, block], axis=0).astype(jnp.bfloat16))
            flat.append(jnp.where(lo_iota == (c & (LANES - 1)), 1.0, 0.0).astype(jnp.bfloat16))
        return acc + lax.dot_general(
            jnp.concatenate(tall, axis=1),
            jnp.concatenate(flat, axis=1),
            (((1,), (1,)), ((), ())),
            preferred_element_type=f32,
        )

    loaded("owner")
    held = jnp.zeros((1, LANES), i32)
    for b in range(n_blk):
        held = jnp.where(lane == owner_ref[b], b, held)
    held_vec[...] = held
    held_copy = pltpu.make_async_copy(held_vec, held_ref, held_sem)
    held_copy.start()

    loaded("rcell")
    inv = lax.fori_loop(0, n_blk // INVERTED, invert, jnp.zeros((2 * n_hi, LANES), f32))
    inv = inv.astype(i32) - 1
    inv_ref[0] = jnp.maximum(inv[:n_hi], 0)
    inv_ref[1] = inv[n_hi:]
    held_copy.wait()

    loaded("count", "state", "dcell", "dweight")
    filled[...] = state_ref[...]

    pl.semaphore_wait(barrier, n_blk - 1 + n_pen - 1)

    def fringe_offset(i):
        return n_blk // 2 + lax.div(i + 1, 2) * (2 * lax.rem(i, 2) - 1)

    def fringe_copy(slot, peer, source):
        return pltpu.make_async_remote_copy(
            src_ref=rows_out.at[slot],
            dst_ref=rows_in.at[source],
            send_sem=fringe_send.at[slot],
            recv_sem=fringe_recv.at[source],
            device_id={"blk": peer},
            device_id_type=MESH,
        )

    def interpolate(q, _):
        peers, blocks, his, los = [], [], [], []
        for u in range(TOGETHER):
            peer = lax.rem(me_b + fringe_offset(q * TOGETHER + u), n_blk)
            block = held_ref[0, peer]
            cells = dcell_ref[block]
            peers.append(peer)
            blocks.append(block)
            his.append(lax.shift_right_logical(cells, 7))
            los.append(cells & (LANES - 1))

        def pick(g, acc):
            acc = [list(one) for one in acc]
            for j in range(depth):
                here = [hi == j * groups + g for hi in his]
                for m in range(nf):
                    table = jnp.broadcast_to(state_ref[m, j : j + 1, lane_group(g)], (8, LANES))
                    for u in range(TOGETHER):
                        acc[u][m] = jnp.where(here[u], lane_pick(table, los[u]), acc[u][m])
            return tuple(tuple(one) for one in acc)

        zero = jnp.zeros((8, LANES), f32)
        acc = lax.fori_loop(0, groups, pick, tuple(tuple(zero for _ in range(nf)) for _ in range(TOGETHER)))
        for u in range(TOGETHER):
            slot = q * TOGETHER + u
            weight = dweight_ref[blocks[u]]
            live = lane < count_ref[blocks[u]]
            for m in range(nf):
                row = jnp.sum(acc[u][m] * weight, axis=0, keepdims=True)
                if m == 0:
                    row = jnp.where(live, row, DEAD)
                rows_out[slot, pl.ds(m, 1), :] = row

            @pl.when(slot < n_blk - 1)
            def _():
                fringe_copy(slot, peers[u], me_b).start()

        return 0

    lax.fori_loop(0, n_blk // TOGETHER, interpolate, 0)

    def place(i, _):
        source = lax.rem(me_b - fringe_offset(i) + n_blk, n_blk)
        fringe_copy(i, source, source).wait_recv()
        block = held_ref[0, source]
        tables = [jnp.broadcast_to(rows_in[source, m : m + 1, :], (depth, LANES)) for m in range(nf)]
        for g in range(groups):
            lanes = slice(g * LANES, (g + 1) * LANES)
            slot = inv_ref[0, g * depth : (g + 1) * depth, :]
            first = lane_pick(tables[0], slot)
            here = (inv_ref[1, g * depth : (g + 1) * depth, :] == block) & (first < 0.5 * DEAD)
            for m in range(nf):
                value = first if m == 0 else lane_pick(tables[m], slot)
                filled[m, :, lanes] = jnp.where(here, value, filled[m, :, lanes])
        return 0

    lax.fori_loop(0, n_blk - 1, place, 0)

    def halo_copy(way, peer):
        return pltpu.make_async_remote_copy(
            src_ref=halo_out.at[way],
            dst_ref=halo_in.at[way],
            send_sem=halo_send.at[way],
            recv_sem=halo_recv.at[way],
            device_id={"pen": peer},
            device_id_type=MESH,
        )

    halo_out[0] = filled[:, depth - 2 :, :]
    halo_out[1] = filled[:, :2, :]
    upward = halo_copy(0, lax.rem(me_p + 1, n_pen))
    downward = halo_copy(1, lax.rem(me_p + n_pen - 1, n_pen))

    @pl.when(me_p < n_pen - 1)
    def _():
        upward.start()

    @pl.when(me_p > 0)
    def _():
        downward.start()

    loaded("prev", "iblank", "speed", "left")
    layer = lax.broadcasted_iota(i32, (depth, pencils), 0)
    keep = iblank_ref[...].astype(f32)

    def wave(m):
        return jnp.concatenate([speed_ref[m * groups + g : m * groups + g + 1, :] for g in range(groups)], axis=1)

    for m in range(nf):
        cur = filled[m]
        upper = jnp.where(layer == depth - 1, 0.0, pltpu.roll(cur, depth - 1, 0))
        upper_two = jnp.where(layer >= depth - 2, 0.0, pltpu.roll(cur, depth - 2, 0))
        lower = jnp.where(layer == 0, 0.0, pltpu.roll(cur, 1, 0))
        lower_two = jnp.where(layer <= 1, 0.0, pltpu.roll(cur, 2, 0))
        r = -(cur - prev_ref[m]) - 0.5 * wave(m) * (upper - lower)
        r = r + 0.25 * (upper - 2.0 * cur + lower)
        r = r - 0.0625 * (upper_two - 4.0 * upper + 6.0 * cur - 4.0 * lower + lower_two)
        r = r - 0.25 * (pltpu.roll(cur, pencils - 1, 1) - pltpu.roll(cur, 1, 1))
        resid[m] = r * keep

    def mix(matrix_ref, values_ref, m, g):
        lanes = slice(g * LANES, (g + 1) * LANES)
        total = None
        for n in range(nf):
            at = (m * nf + n) * groups + g
            term = matrix_ref[at : at + 1, :] * values_ref[n, :, lanes]
            total = term if total is None else total + term
        return total

    def slab_rows(p):
        return pl.ds(pl.multiple_of(p * depth, depth), depth)

    def each_peer(do):
        lax.fori_loop(0, n_a, lambda i, _: do(1 - zh, lax.rem(a + i, n_a)), 0)
        lax.fori_loop(1, n_a, lambda i, _: do(zh, lax.rem(a + i, n_a)), 0)

    def each_source(do):
        lax.fori_loop(1, n_a, lambda i, _: do(zh, lax.rem(a + n_a - i, n_a)), 0)
        lax.fori_loop(0, n_a, lambda i, _: do(1 - zh, lax.rem(a + n_a - i, n_a)), 0)

    def takes_third(half, g):
        return lax.rem(g, 2) == half

    def fwd_copy(message, half, g, source):
        first, lanes, peer = half * 2, lane_group(g), half * n_a + g
        src, dst = (
            lambda: (work.at[0, pl.ds(first, 2), :, lanes], parts_in.at[0, pl.ds(0, 2), source]),
            lambda: (work.at[1, first, :, lanes], parts_in.at[1, 0, source]),
            lambda: (work.at[1, first + 1, :, lanes], parts_in.at[1, 1, source]),
            lambda: (work.at[0, 4, :, lanes], parts_in.at[0, 2, source]),
            lambda: (work.at[1, 4, :, lanes], parts_in.at[1, 2, source]),
        )[message]()
        return pltpu.make_async_remote_copy(
            src_ref=src,
            dst_ref=dst,
            send_sem=fwd_send.at[message, peer],
            recv_sem=fwd_recv.at[message, source],
            device_id={"pen": peer},
            device_id_type=MESH,
        )

    def send_message(message):
        def send(half, g):
            if message < 3:
                fwd_copy(message, half, g, me_p).start()
            else:

                @pl.when(takes_third(half, g))
                def _():
                    fwd_copy(message, half, g, me_p).start()

            return 0

        each_peer(send)

    def keep_part(part):
        for f in range(3):
            field = 4 if f == 2 else zh * 2 + f
            parts_in[part, f, me_p] = work[part, field, :, lane_group(a)]

    for g in range(groups):
        for m in range(nf):
            work[0, m, :, g * LANES : (g + 1) * LANES] = mix(left_ref, resid, m, g)[2 : depth - 2, :]
    send_message(0)
    send_message(3)
    keep_part(0)

    @pl.when(me_p > 0)
    def _():
        upward.wait_recv()

    @pl.when(me_p < n_pen - 1)
    def _():
        downward.wait_recv()

    for m in range(nf):
        low2, low1 = halo_in[0, m, 0:1, :], halo_in[0, m, 1:2, :]
        up1, up2 = halo_in[1, m, 0:1, :], halo_in[1, m, 1:2, :]
        speed = wave(m)
        first = (0.5 + 0.5 * speed) * low1 - 0.0625 * low2
        last = (0.5 - 0.5 * speed) * up1 - 0.0625 * up2
        second, last_but = -0.0625 * low1, -0.0625 * up1
        extra = jnp.where(
            layer == 0,
            first,
            jnp.where(layer == 1, second, jnp.where(layer == depth - 1, last, jnp.where(layer == depth - 2, last_but, 0.0))),
        )
        resid[m] = resid[m] + extra * keep

    for g in range(groups):
        lanes = slice(g * LANES, (g + 1) * LANES)
        for m in range(nf):
            mixed = mix(left_ref, resid, m, g)
            work[1, m, 0:2, lanes] = mixed[0:2, :]
            work[1, m, 2:4, lanes] = mixed[depth - 2 :, :]
    for message in (1, 2, 4):
        send_message(message)
    keep_part(1)

    def fringe_left(i, _):
        fringe_copy(i, me_b, me_b).wait_send()
        return 0

    lax.fori_loop(0, n_blk - 1, fringe_left, 0)

    @pl.when(me_p < n_pen - 1)
    def _():
        upward.wait_send()

    @pl.when(me_p > 0)
    def _():
        downward.wait_send()

    loaded("linv", "right")

    def back_copy(f, peer, half, g):
        field = 4 if f == 2 else half * 2 + f
        return pltpu.make_async_remote_copy(
            src_ref=solved_line.at[f, slab_rows(peer), :],
            dst_ref=solved.at[field, :, lane_group(g)],
            send_sem=back_send.at[f, peer],
            recv_sem=back_recv.at[f, half * n_a + g],
            device_id={"pen": peer},
            device_id_type=MESH,
        )

    def solve(f):
        field = 4 if f == 2 else zh * 2 + f

        def arrive(half, g):
            for message in ((0, 1), (2,), (3, 4))[f]:
                fwd_copy(message, half, g, half * n_a + g).wait_recv()
            return 0

        each_source(arrive)
        for p in range(n_pen):
            work_line[p * depth : p * depth + 2, :] = parts_in[1, f, p, 0:2, :]
            work_line[p * depth + 2 : p * depth + 6, :] = parts_in[0, f, p]
            work_line[p * depth + 6 : (p + 1) * depth, :] = parts_in[1, f, p, 2:4, :]
        solved_line[f] = jnp.dot(
            linv_ref[field], work_line[...], precision=lax.Precision.HIGHEST, preferred_element_type=f32
        )

        def send(half, g):
            back_copy(f, half * n_a + g, zh, a).start()
            return 0

        each_peer(send)
        solved[field, :, lane_group(a)] = solved_line[f, slab_rows(me_p), :]

    solve(0)
    solve(1)

    @pl.when(third)
    def _():
        solve(2)

    def fwd_left(half, g):
        for message in range(3):
            fwd_copy(message, half, g, me_p).wait_send()

        @pl.when(takes_third(half, g))
        def _():
            for message in (3, 4):
                fwd_copy(message, half, g, me_p).wait_send()

        return 0

    each_peer(fwd_left)

    def back_left(half, g):
        for f in range(2):
            back_copy(f, half * n_a + g, zh, a).wait_send()

        @pl.when(third)
        def _():
            back_copy(2, half * n_a + g, zh, a).wait_send()

        return 0

    each_peer(back_left)

    def recv_back(half, g):
        for f in range(2):
            back_copy(f, half * n_a + g, half, g).wait_recv()

        @pl.when(takes_third(half, g))
        def _():
            back_copy(2, half * n_a + g, half, g).wait_recv()

        return 0

    each_source(recv_back)

    for g in range(groups):
        lanes = slice(g * LANES, (g + 1) * LANES)
        for m in range(nf):
            out_ref[m, :, lanes] = filled[m, :, lanes] + keep[:, lanes] * mix(right_ref, solved, m, g)


def solution(mesh):
    n_blk, n_pen = mesh.shape["blk"], mesh.shape["pen"]

    def shards(
        state,
        previous,
        iblank,
        block_owner,
        donor_cell,
        donor_weight,
        send_count,
        recv_cell,
        speed,
        left_vectors,
        right_vectors,
        line_inverse,
    ):
        _, depth, nf, pencils = state.shape
        groups = pencils // LANES
        points = line_inverse.shape[-1]
        cap, donors = recv_cell.shape[-1], donor_cell.shape[-1]
        f32 = jnp.float32
        hbm = pl.BlockSpec(memory_space=pltpu.HBM)
        vmem = pl.BlockSpec(memory_space=pltpu.VMEM)
        dma = pltpu.SemaphoreType.DMA
        out = pl.pallas_call(
            functools.partial(kernel, n_blk, n_pen),
            out_shape=jax.ShapeDtypeStruct((nf, depth, pencils), f32),
            in_specs=[hbm] * 12,
            out_specs=vmem,
            scratch_shapes=[
                pltpu.SMEM((n_blk,), jnp.int32),
                pltpu.SMEM((n_blk,), jnp.int32),
                pltpu.VMEM((nf, depth, pencils), f32),
                pltpu.VMEM((nf, depth, pencils), f32),
                pltpu.VMEM((depth, pencils), jnp.int32),
                pltpu.VMEM((n_blk, donors, cap), jnp.int32),
                pltpu.VMEM((n_blk, donors, cap), f32),
                pltpu.VMEM((n_blk, cap), jnp.int32),
                pltpu.VMEM((nf * groups, LANES), f32),
                pltpu.VMEM((nf * nf * groups, LANES), f32),
                pltpu.VMEM((nf * nf * groups, LANES), f32),
                pltpu.VMEM((nf, points, points), f32),
                dma((12,)),
                pltpu.VMEM((1, LANES), jnp.int32),
                pltpu.SMEM((1, LANES), jnp.int32),
                dma(()),
                pltpu.VMEM((2, groups * depth, LANES), jnp.int32),
                pltpu.VMEM((n_blk, nf, cap), f32),
                pltpu.VMEM((n_blk, nf, cap), f32),
                pltpu.VMEM((nf, depth, pencils), f32),
                pltpu.VMEM((2, nf, 2, pencils), f32),
                pltpu.VMEM((2, nf, 2, pencils), f32),
                pltpu.VMEM((nf, depth, pencils), f32),
                pltpu.VMEM((2, nf, depth // 2, pencils), f32),
                pltpu.VMEM((2, 3, n_pen, depth // 2, LANES), f32),
                pltpu.VMEM((points, LANES), f32),
                pltpu.VMEM((3, points, LANES), f32),
                pltpu.VMEM((nf, depth, pencils), f32),
                dma((n_blk,)),
                dma((n_blk,)),
                dma((2,)),
                dma((2,)),
                dma((5, n_pen)),
                dma((5, n_pen)),
                dma((3, n_pen)),
                dma((3, n_pen)),
            ],
            compiler_params=pltpu.CompilerParams(
                collective_id=0, has_side_effects=True, vmem_limit_bytes=60 * 1024 * 1024
            ),
        )(
            block_owner,
            send_count.reshape(n_blk),
            state[0].transpose(1, 0, 2),
            previous[0].transpose(1, 0, 2),
            iblank[0],
            donor_cell[0, 0].transpose(0, 2, 1),
            donor_weight[0, 0].transpose(0, 2, 1),
            recv_cell[0, 0],
            speed.reshape(nf * groups, LANES),
            left_vectors.reshape(nf * nf * groups, LANES),
            right_vectors.reshape(nf * nf * groups, LANES),
            line_inverse[0],
        )
        return out.transpose(1, 0, 2)[None]

    placed = (
        P("blk", "pen", None, None),
        P("blk", "pen", None, None),
        P("blk", "pen", None),
        P(),
        P("pen", "blk", None, None, None),
        P("pen", "blk", None, None, None),
        P("pen", "blk", None),
        P("pen", "blk", None, None),
        P("blk", None, None),
        P("blk", None, None, None),
        P("blk", None, None, None),
        P("blk", None, None, None),
    )
    return jax.shard_map(
        shards, mesh=mesh, in_specs=placed, out_specs=P("blk", "pen", None, None), check_vma=False
    )
```

```python
import functools

import jax
import jax.numpy as jnp
from jax import lax
from jax.experimental import pallas as pl
from jax.experimental.pallas import tpu as pltpu
from jax.sharding import PartitionSpec as P

MESH = pl.DeviceIdType.MESH
LANES = 128
DEAD = 1e30
WIDE = 256
TOGETHER = 2
PLACED = 4


def split(value):
    high = value.astype(jnp.bfloat16)
    return high, (value - high.astype(jnp.float32)).astype(jnp.bfloat16)


def log2(n):
    assert n & (n - 1) == 0
    return n.bit_length() - 1


def kernel(
    n_blk,
    n_pen,
    owner_hbm,
    count_hbm,
    state_hbm,
    prev_hbm,
    iblank_hbm,
    dcell_hbm,
    dweight_hbm,
    rcell_hbm,
    speed_hbm,
    left_hbm,
    right_hbm,
    linv_hbm,
    out_ref,
    owner_ref,
    count_ref,
    state_ref,
    prev_ref,
    iblank_ref,
    dcell_ref,
    dweight_ref,
    rcell_ref,
    speed_ref,
    left_ref,
    right_ref,
    linv_ref,
    load_sem,
    held_vec,
    held_ref,
    held_sem,
    lo_iota,
    recv_lanes,
    parts,
    placed,
    rows_out,
    rows_in,
    filled,
    halo_out,
    halo_in,
    resid,
    work,
    parts_in,
    work_line,
    solved_line,
    solved,
    linv_in,
    linv_send,
    linv_recv,
    fringe_send,
    fringe_recv,
    halo_send,
    halo_recv,
    fwd_send,
    fwd_recv,
    back_send,
    back_recv,
):
    nf, depth, pencils = state_hbm.shape
    groups = pencils // LANES
    n_a = n_pen // 2
    assert n_a == groups and depth == 8 and nf == 5
    wides = pencils // WIDE
    n_hi = wides * depth
    p_bits, w_bits = log2(pencils), log2(WIDE)
    f32, i32 = jnp.float32, jnp.int32

    me_b = lax.axis_index("blk")
    me_p = lax.axis_index("pen")
    zh = lax.div(me_p, n_a)
    a = lax.rem(me_p, n_a)
    third = lax.rem(a, 2) == zh

    def lane_group(g):
        return pl.ds(pl.multiple_of(g * LANES, LANES), LANES)

    @pl.when(me_p == 0)
    def _():
        halo_in[0] = jnp.zeros(halo_in.shape[1:], f32)

    @pl.when(me_p == n_pen - 1)
    def _():
        halo_in[1] = jnp.zeros(halo_in.shape[1:], f32)

    barrier = pltpu.get_barrier_semaphore()

    partner = lax.rem(me_b + n_blk // 2, n_blk)

    def greet(where):
        pl.semaphore_signal(barrier, inc=1, device_id=where, device_id_type=MESH)

    def greet_blk(off, _):
        greet({"blk": lax.rem(me_b + off, n_blk)})
        return 0

    def greet_lines(off, _):
        greet({"blk": partner, "pen": lax.rem(me_p + off, n_pen)})
        return 0

    lax.fori_loop(1, n_blk, greet_blk, 0)
    lax.fori_loop(1, n_pen, greet_lines, 0)

    greet({"pen": lax.rem(me_p + 1, n_pen)})
    greet({"pen": lax.rem(me_p + n_pen - 1, n_pen)})

    def met():
        pl.semaphore_wait(barrier, n_blk - 1 + n_pen - 1 + 2)

    loads = {}
    for name, source, target in (
        ("rcell", rcell_hbm, rcell_ref),
        ("owner", owner_hbm, owner_ref),
        ("count", count_hbm, count_ref),
        ("state", state_hbm, state_ref),
        ("dcell", dcell_hbm, dcell_ref),
        ("dweight", dweight_hbm, dweight_ref),
        ("prev", prev_hbm, prev_ref),
        ("iblank", iblank_hbm, iblank_ref),
        ("speed", speed_hbm, speed_ref),
        ("left", left_hbm, left_ref),
        ("linv", linv_hbm, linv_ref),
        ("right", right_hbm, right_ref),
    ):
        loads[name] = pltpu.make_async_copy(source, target, load_sem.at[len(loads)])
        loads[name].start()

    def loaded(*names):
        for name in names:
            loads[name].wait()

    lane = lax.broadcasted_iota(i32, (1, LANES), 1)
    lo_iota[...] = lax.broadcasted_iota(i32, (WIDE, LANES), 0).astype(f32).astype(jnp.bfloat16)

    def high_of(cells):
        wide = lax.shift_right_logical(cells, w_bits) & (wides - 1)
        return wide * depth + lax.shift_right_logical(cells, p_bits)

    def pick_lanes(cells):
        low = (cells & (WIDE - 1)).astype(f32).astype(jnp.bfloat16)
        return jnp.where(lo_iota[...] == low, jnp.bfloat16(1), jnp.bfloat16(0))

    loaded("owner")
    held = jnp.zeros((1, LANES), i32)
    for b in range(n_blk):
        held = jnp.where(lane == owner_ref[b], b, held)
    held_vec[...] = held
    held_copy = pltpu.make_async_copy(held_vec, held_ref, held_sem)
    held_copy.start()

    held_copy.wait()

    loaded("count", "state", "dcell", "dweight")
    tiles = [state_ref[m, :, w * WIDE : (w + 1) * WIDE] for m in range(nf) for w in range(wides)]
    n_rows = nf * n_hi
    parts[...] = jnp.concatenate(split(jnp.concatenate(tiles, axis=0)), axis=0)

    def fringe_offset(i):
        return n_blk // 2 + lax.div(i + 1, 2) * (2 * lax.rem(i, 2) - 1)

    def fringe_copy(slot, peer, source):
        return pltpu.make_async_remote_copy(
            src_ref=rows_out.at[slot],
            dst_ref=rows_in.at[source],
            send_sem=fringe_send.at[slot],
            recv_sem=fringe_recv.at[source],
            device_id={"blk": peer},
            device_id_type=MESH,
        )

    hi_iota = lax.broadcasted_iota(i32, (n_hi, LANES), 0)
    donors = dcell_ref.shape[1]

    def interpolate(q, send):
        for u in range(TOGETHER):
            slot = q * TOGETHER + u
            peer = lax.rem(me_b + fringe_offset(slot), n_blk)
            block = held_ref[0, peer]
            cells, weights = dcell_ref[block], dweight_ref[block]
            acc = [None] * nf
            for i in range(0, donors, 2):
                pair = [cells[k : k + 1, :] for k in (i, i + 1)]
                picks = jnp.concatenate([pick_lanes(c) for c in pair], axis=1)
                both = jnp.dot(parts[...], picks, preferred_element_type=f32)
                both = both[:n_rows] + both[n_rows:]
                for k in range(2):
                    weight = jnp.where(hi_iota == high_of(pair[k]), weights[i + k : i + k + 1, :], 0.0)
                    for m in range(nf):
                        term = both[m * n_hi : (m + 1) * n_hi, k * LANES : (k + 1) * LANES] * weight
                        term = sum(term[w * depth : (w + 1) * depth] for w in range(wides))
                        acc[m] = term if acc[m] is None else acc[m] + term
            live = lane < count_ref[block]
            for m in range(nf):
                row = jnp.sum(acc[m], axis=0, keepdims=True)
                if m == 0:
                    row = jnp.where(live, row, DEAD)
                rows_out[slot, pl.ds(m, 1), :] = row

            if send:

                @pl.when(slot < n_blk - 1)
                def _():
                    fringe_copy(slot, peer, me_b).start()

        return 0

    def send_ready(slot, _):
        fringe_copy(slot, lax.rem(me_b + fringe_offset(slot), n_blk), me_b).start()
        return 0

    def inverse_copies():
        def copy(i, field, count):
            return pltpu.make_async_remote_copy(
                src_ref=linv_ref.at[pl.ds(field, count)],
                dst_ref=linv_in.at[pl.ds(2 * i, count)],
                send_sem=linv_send.at[i],
                recv_sem=linv_recv.at[i],
                device_id={"blk": partner},
                device_id_type=MESH,
            )

        return copy(0, zh * 2, 2), copy(1, 4, 1)

    steps = n_blk // TOGETHER
    lax.fori_loop(0, steps // 2, lambda q, _: interpolate(q, False), 0)
    met()
    lax.fori_loop(0, steps // 2 * TOGETHER, send_ready, 0)
    loaded("linv")
    inverses = inverse_copies()
    inverses[0].start()

    @pl.when(third)
    def _():
        inverses[1].start()

    lax.fori_loop(steps // 2, steps, lambda q, _: interpolate(q, True), 0)

    loaded("rcell")

    def receivers(b, _):
        recv_lanes[b] = pick_lanes(rcell_ref[pl.ds(b, 1), :])
        return 0

    lax.fori_loop(0, n_blk, receivers, 0)
    rows_in[me_b] = jnp.full(rows_in.shape[1:], DEAD, f32)

    placed[...] = jnp.zeros_like(placed)

    def place(q, _):
        tall, flat = [], []
        for u in range(PLACED):
            i = q * PLACED + u
            source = lax.rem(me_b - fringe_offset(i) + n_blk, n_blk)

            @pl.when(i < n_blk - 1)
            def _():
                fringe_copy(i, source, source).wait_recv()

            block = held_ref[0, source]
            rows = [rows_in[source, m : m + 1, :] for m in range(nf)]
            here = (hi_iota == high_of(rcell_ref[pl.ds(block, 1), :])) & (rows[0] < 0.5 * DEAD)
            high, low = split(jnp.concatenate([jnp.where(here, row, 0.0) for row in rows], axis=0))
            hit = jnp.where(here, 1.0, 0.0).astype(jnp.bfloat16)
            tall.append(jnp.concatenate([high, low, hit], axis=0))
            flat.append(recv_lanes[block])
        placed[...] += lax.dot_general(
            jnp.concatenate(tall, axis=1),
            jnp.concatenate(flat, axis=1),
            (((1,), (1,)), ((), ())),
            preferred_element_type=f32,
        )
        return 0

    lax.fori_loop(0, n_blk // PLACED, place, 0)
    for m in range(nf):
        for w in range(wides):
            at, lanes = m * n_hi + w * depth, slice(w * WIDE, (w + 1) * WIDE)
            value = placed[at : at + depth, :] + placed[n_rows + at : n_rows + at + depth, :]
            hit = placed[2 * n_rows + w * depth : 2 * n_rows + (w + 1) * depth, :]
            filled[m, :, lanes] = jnp.where(hit > 0.5, value, state_ref[m, :, lanes])

    def halo_copy(way, peer):
        return pltpu.make_async_remote_copy(
            src_ref=halo_out.at[way],
            dst_ref=halo_in.at[way],
            send_sem=halo_send.at[way],
            recv_sem=halo_recv.at[way],
            device_id={"pen": peer},
            device_id_type=MESH,
        )

    halo_out[0] = filled[:, depth - 2 :, :]
    halo_out[1] = filled[:, :2, :]
    upward = halo_copy(0, lax.rem(me_p + 1, n_pen))
    downward = halo_copy(1, lax.rem(me_p + n_pen - 1, n_pen))

    @pl.when(me_p < n_pen - 1)
    def _():
        upward.start()

    @pl.when(me_p > 0)
    def _():
        downward.start()

    loaded("prev", "iblank", "speed", "left")
    layer = lax.broadcasted_iota(i32, (depth, pencils), 0)
    keep = iblank_ref[...].astype(f32)

    def wave(m):
        return jnp.concatenate([speed_ref[m * groups + g : m * groups + g + 1, :] for g in range(groups)], axis=1)

    for m in range(nf):
        cur = filled[m]
        upper = jnp.where(layer == depth - 1, 0.0, pltpu.roll(cur, depth - 1, 0))
        upper_two = jnp.where(layer >= depth - 2, 0.0, pltpu.roll(cur, depth - 2, 0))
        lower = jnp.where(layer == 0, 0.0, pltpu.roll(cur, 1, 0))
        lower_two = jnp.where(layer <= 1, 0.0, pltpu.roll(cur, 2, 0))
        r = -(cur - prev_ref[m]) - 0.5 * wave(m) * (upper - lower)
        r = r + 0.25 * (upper - 2.0 * cur + lower)
        r = r - 0.0625 * (upper_two - 4.0 * upper + 6.0 * cur - 4.0 * lower + lower_two)
        r = r - 0.25 * (pltpu.roll(cur, pencils - 1, 1) - pltpu.roll(cur, 1, 1))
        resid[m] = r * keep

    def mix(matrix_ref, value, m, g):
        total = None
        for n in range(nf):
            at = (m * nf + n) * groups + g
            term = matrix_ref[at : at + 1, :] * value(n, g)
            total = term if total is None else total + term
        return total

    def resid_at(n, g):
        return resid[n, :, g * LANES : (g + 1) * LANES]

    def place_of(m, g):
        return (g % 2, g, 2) if m == 4 else (m // 2, g, m % 2)

    def each_peer(do):
        lax.fori_loop(0, n_a, lambda i, _: do(1 - zh, lax.rem(a + i, n_a)), 0)
        lax.fori_loop(0, n_a, lambda i, _: do(zh, lax.rem(a + i, n_a)), 0)

    def each_source(do):
        lax.fori_loop(0, n_a, lambda i, _: do(zh, lax.rem(a + n_a - i, n_a)), 0)
        lax.fori_loop(0, n_a, lambda i, _: do(1 - zh, lax.rem(a + n_a - i, n_a)), 0)

    def takes_third(half, g):
        return lax.rem(g, 2) == half

    def sized(more, do):
        @pl.when(more)
        def _():
            do(3)

        @pl.when(jnp.logical_not(more))
        def _():
            do(2)

        return 0

    def fwd_copy(part, half, g, source, count):
        peer = half * n_a + g
        return pltpu.make_async_remote_copy(
            src_ref=work.at[part, half, g, pl.ds(0, count)],
            dst_ref=parts_in.at[part, source, pl.ds(0, count)],
            send_sem=fwd_send.at[part, peer],
            recv_sem=fwd_recv.at[part, source],
            device_id={"blk": partner, "pen": peer},
            device_id_type=MESH,
        )

    def send_part(part):
        each_peer(
            lambda half, g: sized(
                takes_third(half, g), lambda count: fwd_copy(part, half, g, me_p, count).start()
            )
        )

    for g in range(groups):
        for m in range(nf):
            work[(0, *place_of(m, g))] = mix(left_ref, resid_at, m, g)[2 : depth - 2, :]
    send_part(0)

    @pl.when(me_p > 0)
    def _():
        upward.wait_recv()

    @pl.when(me_p < n_pen - 1)
    def _():
        downward.wait_recv()

    for m in range(nf):
        low2, low1 = halo_in[0, m, 0:1, :], halo_in[0, m, 1:2, :]
        up1, up2 = halo_in[1, m, 0:1, :], halo_in[1, m, 1:2, :]
        speed = wave(m)
        first = (0.5 + 0.5 * speed) * low1 - 0.0625 * low2
        last = (0.5 - 0.5 * speed) * up1 - 0.0625 * up2
        second, last_but = -0.0625 * low1, -0.0625 * up1
        extra = jnp.where(
            layer == 0,
            first,
            jnp.where(layer == 1, second, jnp.where(layer == depth - 1, last, jnp.where(layer == depth - 2, last_but, 0.0))),
        )
        resid[m] = resid[m] + extra * keep

    for g in range(groups):
        for m in range(nf):
            half, at, f = place_of(m, g)
            mixed = mix(left_ref, resid_at, m, g)
            work[1, half, at, f, 0:2, :] = mixed[0:2, :]
            work[1, half, at, f, 2:4, :] = mixed[depth - 2 :, :]
    send_part(1)

    def fringe_left(i, _):
        fringe_copy(i, me_b, me_b).wait_send()
        return 0

    lax.fori_loop(0, n_blk - 1, fringe_left, 0)

    @pl.when(me_p < n_pen - 1)
    def _():
        upward.wait_send()

    @pl.when(me_p > 0)
    def _():
        downward.wait_send()

    loaded("right")
    inverses[0].wait_recv()

    @pl.when(third)
    def _():
        inverses[1].wait_recv()

    def arrive(half, g):
        source = half * n_a + g
        for part in range(2):
            sized(third, lambda count: fwd_copy(part, half, g, source, count).wait_recv())
        return 0

    each_source(arrive)

    def solve(f):
        for p in range(n_pen):
            work_line[p * depth : p * depth + 2, :] = parts_in[1, p, f, 0:2, :]
            work_line[p * depth + 2 : p * depth + 6, :] = parts_in[0, p, f]
            work_line[p * depth + 6 : (p + 1) * depth, :] = parts_in[1, p, f, 2:4, :]
        inv_high, inv_low = split(linv_in[f])
        line_high, line_low = split(work_line[...])
        line = jnp.dot(
            jnp.concatenate([inv_high, inv_high, inv_low], axis=1),
            jnp.concatenate([line_high, line_low, line_high], axis=0),
            preferred_element_type=f32,
        )
        for p in range(n_pen):
            solved_line[p, f] = line[p * depth : (p + 1) * depth, :]

    solve(0)
    solve(1)

    @pl.when(third)
    def _():
        solve(2)

    def back_copy(peer, half, g, count):
        return pltpu.make_async_remote_copy(
            src_ref=solved_line.at[peer, pl.ds(0, count)],
            dst_ref=solved.at[half, g, pl.ds(0, count)],
            send_sem=back_send.at[peer],
            recv_sem=back_recv.at[half * n_a + g],
            device_id={"blk": partner, "pen": peer},
            device_id_type=MESH,
        )

    each_peer(
        lambda half, g: sized(third, lambda count: back_copy(half * n_a + g, zh, a, count).start())
    )

    inverses[0].wait_send()

    @pl.when(third)
    def _():
        inverses[1].wait_send()

    def left(half, g):
        for part in range(2):
            sized(takes_third(half, g), lambda count: fwd_copy(part, half, g, me_p, count).wait_send())
        return sized(third, lambda count: back_copy(half * n_a + g, zh, a, count).wait_send())

    each_peer(left)
    each_source(
        lambda half, g: sized(
            takes_third(half, g), lambda count: back_copy(half * n_a + g, half, g, count).wait_recv()
        )
    )

    def solved_at(n, g):
        return solved[place_of(n, g)]

    for g in range(groups):
        lanes = slice(g * LANES, (g + 1) * LANES)
        for m in range(nf):
            out_ref[m, :, lanes] = filled[m, :, lanes] + keep[:, lanes] * mix(right_ref, solved_at, m, g)


def solution(mesh):
    n_blk, n_pen = mesh.shape["blk"], mesh.shape["pen"]

    def shards(
        state,
        previous,
        iblank,
        block_owner,
        donor_cell,
        donor_weight,
        send_count,
        recv_cell,
        speed,
        left_vectors,
        right_vectors,
        line_inverse,
    ):
        _, depth, nf, pencils = state.shape
        groups, n_hi = pencils // LANES, pencils // WIDE * depth
        points = line_inverse.shape[-1]
        cap, donors = recv_cell.shape[-1], donor_cell.shape[-1]
        f32 = jnp.float32
        hbm = pl.BlockSpec(memory_space=pltpu.HBM)
        vmem = pl.BlockSpec(memory_space=pltpu.VMEM)
        dma = pltpu.SemaphoreType.DMA
        out = pl.pallas_call(
            functools.partial(kernel, n_blk, n_pen),
            out_shape=jax.ShapeDtypeStruct((nf, depth, pencils), f32),
            in_specs=[hbm] * 12,
            out_specs=vmem,
            scratch_shapes=[
                pltpu.SMEM((n_blk,), jnp.int32),
                pltpu.SMEM((n_blk,), jnp.int32),
                pltpu.VMEM((nf, depth, pencils), f32),
                pltpu.VMEM((nf, depth, pencils), f32),
                pltpu.VMEM((depth, pencils), jnp.int32),
                pltpu.VMEM((n_blk, donors, cap), jnp.int32),
                pltpu.VMEM((n_blk, donors, cap), f32),
                pltpu.VMEM((n_blk, cap), jnp.int32),
                pltpu.VMEM((nf * groups, LANES), f32),
                pltpu.VMEM((nf * nf * groups, LANES), f32),
                pltpu.VMEM((nf * nf * groups, LANES), f32),
                pltpu.VMEM((nf, points, points), f32),
                dma((12,)),
                pltpu.VMEM((1, LANES), jnp.int32),
                pltpu.SMEM((1, LANES), jnp.int32),
                dma(()),
                pltpu.VMEM((WIDE, LANES), jnp.bfloat16),
                pltpu.VMEM((n_blk, WIDE, LANES), jnp.bfloat16),
                pltpu.VMEM((2 * nf * n_hi, WIDE), jnp.bfloat16),
                pltpu.VMEM(((2 * nf + 1) * n_hi, WIDE), f32),
                pltpu.VMEM((n_blk, nf, cap), f32),
                pltpu.VMEM((n_blk, nf, cap), f32),
                pltpu.VMEM((nf, depth, pencils), f32),
                pltpu.VMEM((2, nf, 2, pencils), f32),
                pltpu.VMEM((2, nf, 2, pencils), f32),
                pltpu.VMEM((nf, depth, pencils), f32),
                pltpu.VMEM((2, 2, groups, 3, depth // 2, LANES), f32),
                pltpu.VMEM((2, n_pen, 3, depth // 2, LANES), f32),
                pltpu.VMEM((points, LANES), f32),
                pltpu.VMEM((n_pen, 3, depth, LANES), f32),
                pltpu.VMEM((2, groups, 3, depth, LANES), f32),
                pltpu.VMEM((3, points, points), f32),
                dma((2,)),
                dma((2,)),
                dma((n_blk,)),
                dma((n_blk,)),
                dma((2,)),
                dma((2,)),
                dma((2, n_pen)),
                dma((2, n_pen)),
                dma((n_pen,)),
                dma((n_pen,)),
            ],
            compiler_params=pltpu.CompilerParams(
                collective_id=0, has_side_effects=True, vmem_limit_bytes=60 * 1024 * 1024
            ),
        )(
            block_owner,
            send_count.reshape(n_blk),
            state[0].transpose(1, 0, 2),
            previous[0].transpose(1, 0, 2),
            iblank[0],
            donor_cell[0, 0].transpose(0, 2, 1),
            donor_weight[0, 0].transpose(0, 2, 1),
            recv_cell[0, 0],
            speed.reshape(nf * groups, LANES),
            left_vectors.reshape(nf * nf * groups, LANES),
            right_vectors.reshape(nf * nf * groups, LANES),
            line_inverse[0],
        )
        return out.transpose(1, 0, 2)[None]

    placed = (
        P("blk", "pen", None, None),
        P("blk", "pen", None, None),
        P("blk", "pen", None),
        P(),
        P("pen", "blk", None, None, None),
        P("pen", "blk", None, None, None),
        P("pen", "blk", None),
        P("pen", "blk", None, None),
        P("blk", None, None),
        P("blk", None, None, None),
        P("blk", None, None, None),
        P("blk", None, None, None),
    )
    return jax.shard_map(
        shards, mesh=mesh, in_specs=placed, out_specs=P("blk", "pen", None, None), check_vma=False
    )
```

```python
import functools

import jax
import jax.numpy as jnp
from jax import lax
from jax.experimental import pallas as pl
from jax.experimental.pallas import tpu as pltpu
from jax.sharding import PartitionSpec as P

MESH = pl.DeviceIdType.MESH
LANES = 128
DEAD = 1e30
WIDE = 256
TOGETHER = 4
PLACED = 4


def split(value):
    high = value.astype(jnp.bfloat16)
    return high, (value - high.astype(jnp.float32)).astype(jnp.bfloat16)


def log2(n):
    assert n & (n - 1) == 0
    return n.bit_length() - 1


def kernel(
    n_blk,
    n_pen,
    owner_hbm,
    count_hbm,
    state_hbm,
    prev_hbm,
    iblank_hbm,
    dcell_hbm,
    dweight_hbm,
    rcell_hbm,
    speed_hbm,
    left_hbm,
    right_hbm,
    linv_hbm,
    out_ref,
    owner_ref,
    count_ref,
    state_ref,
    prev_ref,
    iblank_ref,
    dcell_ref,
    dweight_ref,
    rcell_ref,
    speed_ref,
    left_ref,
    right_ref,
    linv_ref,
    load_sem,
    held_vec,
    held_ref,
    held_sem,
    lo_iota,
    recv_lanes,
    parts,
    placed,
    rows_out,
    rows_in,
    filled,
    halo_out,
    halo_in,
    resid,
    work,
    parts_in,
    work_line,
    solved_line,
    solved,
    fringe_send,
    fringe_recv,
    halo_send,
    halo_recv,
    fwd_send,
    fwd_recv,
    back_send,
    back_recv,
):
    nf, depth, pencils = state_hbm.shape
    groups = pencils // LANES
    n_a = n_pen // 2
    assert n_a == groups and depth == 8 and nf == 5
    wides = pencils // WIDE
    n_hi = wides * depth
    p_bits, w_bits = log2(pencils), log2(WIDE)
    f32, i32 = jnp.float32, jnp.int32

    me_b = lax.axis_index("blk")
    me_p = lax.axis_index("pen")
    zh = lax.div(me_p, n_a)
    a = lax.rem(me_p, n_a)
    third = lax.rem(a, 2) == zh

    def lane_group(g):
        return pl.ds(pl.multiple_of(g * LANES, LANES), LANES)

    loads = {}
    for name, source, target in (
        ("owner", owner_hbm, owner_ref),
        ("state", state_hbm, state_ref),
        ("dcell", dcell_hbm, dcell_ref),
        ("dweight", dweight_hbm, dweight_ref),
        ("count", count_hbm, count_ref),
        ("rcell", rcell_hbm, rcell_ref),
        ("prev", prev_hbm, prev_ref),
        ("iblank", iblank_hbm, iblank_ref),
        ("speed", speed_hbm, speed_ref),
        ("left", left_hbm, left_ref),
        ("linv", linv_hbm, linv_ref),
        ("right", right_hbm, right_ref),
    ):
        loads[name] = pltpu.make_async_copy(source, target, load_sem.at[len(loads)])
        loads[name].start()

    def loaded(*names):
        for name in names:
            loads[name].wait()

    @pl.when(me_p == 0)
    def _():
        halo_in[0] = jnp.zeros(halo_in.shape[1:], f32)

    @pl.when(me_p == n_pen - 1)
    def _():
        halo_in[1] = jnp.zeros(halo_in.shape[1:], f32)

    barrier = pltpu.get_barrier_semaphore()

    def greet(where):
        pl.semaphore_signal(barrier, inc=1, device_id=where, device_id_type=MESH)
        return 0

    lax.fori_loop(1, n_blk, lambda off, _: greet({"blk": lax.rem(me_b + off, n_blk)}), 0)
    lax.fori_loop(1, n_pen, lambda off, _: greet({"pen": lax.rem(me_p + off, n_pen)}), 0)

    def met():
        pl.semaphore_wait(barrier, n_blk - 1 + n_pen - 1)

    lane = lax.broadcasted_iota(i32, (1, LANES), 1)
    lo_iota[...] = lax.broadcasted_iota(i32, (WIDE, LANES), 0).astype(f32).astype(jnp.bfloat16)

    def high_of(cells):
        wide = lax.shift_right_logical(cells, w_bits) & (wides - 1)
        return wide * depth + lax.shift_right_logical(cells, p_bits)

    def pick_lanes(cells):
        low = (cells & (WIDE - 1)).astype(f32).astype(jnp.bfloat16)
        return jnp.where(lo_iota[...] == low, jnp.bfloat16(1), jnp.bfloat16(0))

    loaded("owner")
    held = jnp.zeros((1, LANES), i32)
    for b in range(n_blk):
        held = jnp.where(lane == owner_ref[b], b, held)
    held_vec[...] = held
    held_copy = pltpu.make_async_copy(held_vec, held_ref, held_sem)
    held_copy.start()

    held_copy.wait()

    loaded("count", "state", "dcell", "dweight")
    tiles = [state_ref[m, :, w * WIDE : (w + 1) * WIDE] for m in range(nf) for w in range(wides)]
    n_rows = nf * n_hi
    parts[...] = jnp.concatenate(split(jnp.concatenate(tiles, axis=0)), axis=0)

    def fringe_offset(i):
        return n_blk // 2 + lax.div(i + 1, 2) * (2 * lax.rem(i, 2) - 1)

    def fringe_copy(slot, peer, source):
        return pltpu.make_async_remote_copy(
            src_ref=rows_out.at[slot],
            dst_ref=rows_in.at[source],
            send_sem=fringe_send.at[slot],
            recv_sem=fringe_recv.at[source],
            device_id={"blk": peer},
            device_id_type=MESH,
        )

    hi_iota = lax.broadcasted_iota(i32, (n_hi, LANES), 0)
    donors = dcell_ref.shape[1]

    def interpolate(q, send):
        for u in range(TOGETHER):
            slot = q * TOGETHER + u
            peer = lax.rem(me_b + fringe_offset(slot), n_blk)
            block = held_ref[0, peer]
            cells, weights = dcell_ref[block], dweight_ref[block]
            acc = [None] * nf
            for i in range(0, donors, 2):
                pair = [cells[k : k + 1, :] for k in (i, i + 1)]
                picks = jnp.concatenate([pick_lanes(c) for c in pair], axis=1)
                both = jnp.dot(parts[...], picks, preferred_element_type=f32)
                both = both[:n_rows] + both[n_rows:]
                for k in range(2):
                    weight = jnp.where(hi_iota == high_of(pair[k]), weights[i + k : i + k + 1, :], 0.0)
                    for m in range(nf):
                        term = both[m * n_hi : (m + 1) * n_hi, k * LANES : (k + 1) * LANES] * weight
                        term = sum(term[w * depth : (w + 1) * depth] for w in range(wides))
                        acc[m] = term if acc[m] is None else acc[m] + term
            live = lane < count_ref[block]
            for m in range(nf):
                row = jnp.sum(acc[m], axis=0, keepdims=True)
                if m == 0:
                    row = jnp.where(live, row, DEAD)
                rows_out[slot, pl.ds(m, 1), :] = row

        if send:
            for u in range(TOGETHER - 1):
                send_ready(q * TOGETHER + u, 0)
            last = q * TOGETHER + TOGETHER - 1

            @pl.when(last < n_blk - 1)
            def _():
                send_ready(last, 0)

        return 0

    def send_ready(slot, _):
        fringe_copy(slot, lax.rem(me_b + fringe_offset(slot), n_blk), me_b).start()
        return 0

    steps = n_blk // TOGETHER
    lax.fori_loop(0, steps // 2, lambda q, _: interpolate(q, False), 0)
    met()
    lax.fori_loop(0, steps // 2 * TOGETHER, send_ready, 0)
    lax.fori_loop(steps // 2, steps, lambda q, _: interpolate(q, True), 0)

    loaded("rcell")

    def receivers(b, _):
        recv_lanes[b] = pick_lanes(rcell_ref[pl.ds(b, 1), :])
        return 0

    lax.fori_loop(0, n_blk, receivers, 0)
    rows_in[me_b] = jnp.full(rows_in.shape[1:], DEAD, f32)

    placed[...] = jnp.zeros_like(placed)

    def place(q, _):
        sources = [lax.rem(me_b - fringe_offset(q * PLACED + u) + n_blk, n_blk) for u in range(PLACED)]
        for u in range(PLACED - 1):
            fringe_copy(q * PLACED + u, sources[u], sources[u]).wait_recv()
        last = q * PLACED + PLACED - 1

        @pl.when(last < n_blk - 1)
        def _():
            fringe_copy(last, sources[-1], sources[-1]).wait_recv()

        tall, flat = [], []
        for source in sources:
            block = held_ref[0, source]
            rows = [rows_in[source, m : m + 1, :] for m in range(nf)]
            here = (hi_iota == high_of(rcell_ref[pl.ds(block, 1), :])) & (rows[0] < 0.5 * DEAD)
            high, low = split(jnp.concatenate([jnp.where(here, row, 0.0) for row in rows], axis=0))
            hit = jnp.where(here, 1.0, 0.0).astype(jnp.bfloat16)
            tall.append(jnp.concatenate([high, low, hit], axis=0))
            flat.append(recv_lanes[block])
        placed[...] += lax.dot_general(
            jnp.concatenate(tall, axis=1),
            jnp.concatenate(flat, axis=1),
            (((1,), (1,)), ((), ())),
            preferred_element_type=f32,
        )
        return 0

    lax.fori_loop(0, n_blk // PLACED, place, 0)
    for m in range(nf):
        for w in range(wides):
            at, lanes = m * n_hi + w * depth, slice(w * WIDE, (w + 1) * WIDE)
            value = placed[at : at + depth, :] + placed[n_rows + at : n_rows + at + depth, :]
            hit = placed[2 * n_rows + w * depth : 2 * n_rows + (w + 1) * depth, :]
            filled[m, :, lanes] = jnp.where(hit > 0.5, value, state_ref[m, :, lanes])

    def halo_copy(way, peer):
        return pltpu.make_async_remote_copy(
            src_ref=halo_out.at[way],
            dst_ref=halo_in.at[way],
            send_sem=halo_send.at[way],
            recv_sem=halo_recv.at[way],
            device_id={"pen": peer},
            device_id_type=MESH,
        )

    halo_out[0] = filled[:, depth - 2 :, :]
    halo_out[1] = filled[:, :2, :]
    upward = halo_copy(0, lax.rem(me_p + 1, n_pen))
    downward = halo_copy(1, lax.rem(me_p + n_pen - 1, n_pen))

    @pl.when(me_p < n_pen - 1)
    def _():
        upward.start()

    @pl.when(me_p > 0)
    def _():
        downward.start()

    loaded("prev", "iblank", "speed", "left")
    layer = lax.broadcasted_iota(i32, (depth, pencils), 0)
    keep = iblank_ref[...].astype(f32)

    def wave(m):
        return jnp.concatenate([speed_ref[m * groups + g : m * groups + g + 1, :] for g in range(groups)], axis=1)

    for m in range(nf):
        cur = filled[m]
        upper = jnp.where(layer == depth - 1, 0.0, pltpu.roll(cur, depth - 1, 0))
        upper_two = jnp.where(layer >= depth - 2, 0.0, pltpu.roll(cur, depth - 2, 0))
        lower = jnp.where(layer == 0, 0.0, pltpu.roll(cur, 1, 0))
        lower_two = jnp.where(layer <= 1, 0.0, pltpu.roll(cur, 2, 0))
        r = -(cur - prev_ref[m]) - 0.5 * wave(m) * (upper - lower)
        r = r + 0.25 * (upper - 2.0 * cur + lower)
        r = r - 0.0625 * (upper_two - 4.0 * upper + 6.0 * cur - 4.0 * lower + lower_two)
        r = r - 0.25 * (pltpu.roll(cur, pencils - 1, 1) - pltpu.roll(cur, 1, 1))
        resid[m] = r * keep

    def mix(matrix_ref, value, m, g):
        total = None
        for n in range(nf):
            at = (m * nf + n) * groups + g
            term = matrix_ref[at : at + 1, :] * value(n, g)
            total = term if total is None else total + term
        return total

    def resid_at(n, g):
        return resid[n, :, g * LANES : (g + 1) * LANES]

    def place_of(m, g):
        return (g % 2, g, 2) if m == 4 else (m // 2, g, m % 2)

    def each_peer(do):
        lax.fori_loop(0, n_a, lambda i, _: do(1 - zh, lax.rem(a + i, n_a)), 0)
        lax.fori_loop(1, n_a, lambda i, _: do(zh, lax.rem(a + i, n_a)), 0)

    def each_source(do):
        lax.fori_loop(1, n_a, lambda i, _: do(zh, lax.rem(a + n_a - i, n_a)), 0)
        lax.fori_loop(0, n_a, lambda i, _: do(1 - zh, lax.rem(a + n_a - i, n_a)), 0)

    def takes_third(half, g):
        return lax.rem(g, 2) == half

    def sized(more, do):
        @pl.when(more)
        def _():
            do(3)

        @pl.when(jnp.logical_not(more))
        def _():
            do(2)

        return 0

    def fwd_copy(part, half, g, source, count):
        peer = half * n_a + g
        return pltpu.make_async_remote_copy(
            src_ref=work.at[part, half, g, pl.ds(0, count)],
            dst_ref=parts_in.at[part, source, pl.ds(0, count)],
            send_sem=fwd_send.at[part, peer],
            recv_sem=fwd_recv.at[part, source],
            device_id={"pen": peer},
            device_id_type=MESH,
        )

    def send_part(part):
        each_peer(
            lambda half, g: sized(
                takes_third(half, g), lambda count: fwd_copy(part, half, g, me_p, count).start()
            )
        )

        def keep_own(count):
            parts_in[part, me_p, 0:count] = work[part, zh, a, 0:count]

        sized(third, keep_own)

    for g in range(groups):
        for m in range(nf):
            work[(0, *place_of(m, g))] = mix(left_ref, resid_at, m, g)[2 : depth - 2, :]
    send_part(0)

    @pl.when(me_p > 0)
    def _():
        upward.wait_recv()

    @pl.when(me_p < n_pen - 1)
    def _():
        downward.wait_recv()

    for m in range(nf):
        low2, low1 = halo_in[0, m, 0:1, :], halo_in[0, m, 1:2, :]
        up1, up2 = halo_in[1, m, 0:1, :], halo_in[1, m, 1:2, :]
        speed = wave(m)
        first = (0.5 + 0.5 * speed) * low1 - 0.0625 * low2
        last = (0.5 - 0.5 * speed) * up1 - 0.0625 * up2
        second, last_but = -0.0625 * low1, -0.0625 * up1
        extra = jnp.where(
            layer == 0,
            first,
            jnp.where(layer == 1, second, jnp.where(layer == depth - 1, last, jnp.where(layer == depth - 2, last_but, 0.0))),
        )
        resid[m] = resid[m] + extra * keep

    for g in range(groups):
        for m in range(nf):
            half, at, f = place_of(m, g)
            mixed = mix(left_ref, resid_at, m, g)
            work[1, half, at, f, 0:2, :] = mixed[0:2, :]
            work[1, half, at, f, 2:4, :] = mixed[depth - 2 :, :]
    send_part(1)

    def fringe_left(i, _):
        fringe_copy(i, me_b, me_b).wait_send()
        return 0

    lax.fori_loop(0, n_blk - 1, fringe_left, 0)

    @pl.when(me_p < n_pen - 1)
    def _():
        upward.wait_send()

    @pl.when(me_p > 0)
    def _():
        downward.wait_send()

    loaded("linv", "right")
    def arrive(half, g):
        source = half * n_a + g
        for part in range(2):
            sized(third, lambda count: fwd_copy(part, half, g, source, count).wait_recv())
        return 0

    each_source(arrive)

    def solve(f):
        for p in range(n_pen):
            work_line[p * depth : p * depth + 2, :] = parts_in[1, p, f, 0:2, :]
            work_line[p * depth + 2 : p * depth + 6, :] = parts_in[0, p, f]
            work_line[p * depth + 6 : (p + 1) * depth, :] = parts_in[1, p, f, 2:4, :]
        inv_high, inv_low = split(linv_ref[4 if f == 2 else zh * 2 + f])
        line_high, line_low = split(work_line[...])
        line = jnp.dot(
            jnp.concatenate([inv_high, inv_high, inv_low], axis=1),
            jnp.concatenate([line_high, line_low, line_high], axis=0),
            preferred_element_type=f32,
        )
        for p in range(n_pen):
            solved_line[p, f] = line[p * depth : (p + 1) * depth, :]

    solve(0)
    solve(1)

    @pl.when(third)
    def _():
        solve(2)

    def back_copy(peer, half, g, count):
        return pltpu.make_async_remote_copy(
            src_ref=solved_line.at[peer, pl.ds(0, count)],
            dst_ref=solved.at[half, g, pl.ds(0, count)],
            send_sem=back_send.at[peer],
            recv_sem=back_recv.at[half * n_a + g],
            device_id={"pen": peer},
            device_id_type=MESH,
        )

    each_peer(
        lambda half, g: sized(third, lambda count: back_copy(half * n_a + g, zh, a, count).start())
    )

    def keep_solved(count):
        solved[zh, a, 0:count] = solved_line[me_p, 0:count]

    sized(third, keep_solved)

    def left(half, g):
        for part in range(2):
            sized(takes_third(half, g), lambda count: fwd_copy(part, half, g, me_p, count).wait_send())
        return sized(third, lambda count: back_copy(half * n_a + g, zh, a, count).wait_send())

    each_peer(left)
    each_source(
        lambda half, g: sized(
            takes_third(half, g), lambda count: back_copy(half * n_a + g, half, g, count).wait_recv()
        )
    )

    def solved_at(n, g):
        return solved[place_of(n, g)]

    for g in range(groups):
        lanes = slice(g * LANES, (g + 1) * LANES)
        for m in range(nf):
            out_ref[m, :, lanes] = filled[m, :, lanes] + keep[:, lanes] * mix(right_ref, solved_at, m, g)


def solution(mesh):
    n_blk, n_pen = mesh.shape["blk"], mesh.shape["pen"]

    def shards(
        state,
        previous,
        iblank,
        block_owner,
        donor_cell,
        donor_weight,
        send_count,
        recv_cell,
        speed,
        left_vectors,
        right_vectors,
        line_inverse,
    ):
        _, depth, nf, pencils = state.shape
        groups, n_hi = pencils // LANES, pencils // WIDE * depth
        points = line_inverse.shape[-1]
        cap, donors = recv_cell.shape[-1], donor_cell.shape[-1]
        f32 = jnp.float32
        hbm = pl.BlockSpec(memory_space=pltpu.HBM)
        vmem = pl.BlockSpec(memory_space=pltpu.VMEM)
        dma = pltpu.SemaphoreType.DMA
        out = pl.pallas_call(
            functools.partial(kernel, n_blk, n_pen),
            out_shape=jax.ShapeDtypeStruct((nf, depth, pencils), f32),
            in_specs=[hbm] * 12,
            out_specs=vmem,
            scratch_shapes=[
                pltpu.SMEM((n_blk,), jnp.int32),
                pltpu.SMEM((n_blk,), jnp.int32),
                pltpu.VMEM((nf, depth, pencils), f32),
                pltpu.VMEM((nf, depth, pencils), f32),
                pltpu.VMEM((depth, pencils), jnp.int32),
                pltpu.VMEM((n_blk, donors, cap), jnp.int32),
                pltpu.VMEM((n_blk, donors, cap), f32),
                pltpu.VMEM((n_blk, cap), jnp.int32),
                pltpu.VMEM((nf * groups, LANES), f32),
                pltpu.VMEM((nf * nf * groups, LANES), f32),
                pltpu.VMEM((nf * nf * groups, LANES), f32),
                pltpu.VMEM((nf, points, points), f32),
                dma((12,)),
                pltpu.VMEM((1, LANES), jnp.int32),
                pltpu.SMEM((1, LANES), jnp.int32),
                dma(()),
                pltpu.VMEM((WIDE, LANES), jnp.bfloat16),
                pltpu.VMEM((n_blk, WIDE, LANES), jnp.bfloat16),
                pltpu.VMEM((2 * nf * n_hi, WIDE), jnp.bfloat16),
                pltpu.VMEM(((2 * nf + 1) * n_hi, WIDE), f32),
                pltpu.VMEM((n_blk, nf, cap), f32),
                pltpu.VMEM((n_blk, nf, cap), f32),
                pltpu.VMEM((nf, depth, pencils), f32),
                pltpu.VMEM((2, nf, 2, pencils), f32),
                pltpu.VMEM((2, nf, 2, pencils), f32),
                pltpu.VMEM((nf, depth, pencils), f32),
                pltpu.VMEM((2, 2, groups, 3, depth // 2, LANES), f32),
                pltpu.VMEM((2, n_pen, 3, depth // 2, LANES), f32),
                pltpu.VMEM((points, LANES), f32),
                pltpu.VMEM((n_pen, 3, depth, LANES), f32),
                pltpu.VMEM((2, groups, 3, depth, LANES), f32),
                dma((n_blk,)),
                dma((n_blk,)),
                dma((2,)),
                dma((2,)),
                dma((2, n_pen)),
                dma((2, n_pen)),
                dma((n_pen,)),
                dma((n_pen,)),
            ],
            compiler_params=pltpu.CompilerParams(
                collective_id=0, has_side_effects=True, vmem_limit_bytes=60 * 1024 * 1024
            ),
        )(
            block_owner,
            send_count.reshape(n_blk),
            state[0].transpose(1, 0, 2),
            previous[0].transpose(1, 0, 2),
            iblank[0],
            donor_cell[0, 0].transpose(0, 2, 1),
            donor_weight[0, 0].transpose(0, 2, 1),
            recv_cell[0, 0],
            speed.reshape(nf * groups, LANES),
            left_vectors.reshape(nf * nf * groups, LANES),
            right_vectors.reshape(nf * nf * groups, LANES),
            line_inverse[0],
        )
        return out.transpose(1, 0, 2)[None]

    placed = (
        P("blk", "pen", None, None),
        P("blk", "pen", None, None),
        P("blk", "pen", None),
        P(),
        P("pen", "blk", None, None, None),
        P("pen", "blk", None, None, None),
        P("pen", "blk", None),
        P("pen", "blk", None, None),
        P("blk", None, None),
        P("blk", None, None, None),
        P("blk", None, None, None),
        P("blk", None, None, None),
    )
    return jax.shard_map(
        shards, mesh=mesh, in_specs=placed, out_specs=P("blk", "pen", None, None), check_vma=False
    )
```

```python
import functools

import jax
import jax.numpy as jnp
from jax import lax
from jax.experimental import pallas as pl
from jax.experimental.pallas import tpu as pltpu
from jax.sharding import PartitionSpec as P

MESH = pl.DeviceIdType.MESH
LANES = 128
DEAD = 1e30
WIDE = 256
TOGETHER = 4
PLACED = 4


def split(value):
    high = value.astype(jnp.bfloat16)
    return high, (value - high.astype(jnp.float32)).astype(jnp.bfloat16)


def log2(n):
    assert n & (n - 1) == 0
    return n.bit_length() - 1


def kernel(
    n_blk,
    n_pen,
    owner_hbm,
    count_hbm,
    state_hbm,
    prev_hbm,
    iblank_hbm,
    dcell_hbm,
    dweight_hbm,
    rcell_hbm,
    speed_hbm,
    left_hbm,
    right_hbm,
    linv_hbm,
    out_ref,
    owner_ref,
    count_ref,
    state_ref,
    prev_ref,
    iblank_ref,
    dcell_ref,
    dweight_ref,
    rcell_ref,
    speed_ref,
    left_ref,
    right_ref,
    linv_ref,
    load_sem,
    held_vec,
    held_ref,
    held_sem,
    lo_iota,
    recv_lanes,
    parts,
    placed,
    rows_out,
    rows_in,
    filled,
    halo_out,
    halo_in,
    resid,
    work,
    parts_in,
    work_line,
    solved_line,
    solved,
    fringe_send,
    fringe_recv,
    halo_send,
    halo_recv,
    fwd_send,
    fwd_recv,
    back_send,
    back_recv,
):
    nf, depth, pencils = state_hbm.shape
    groups = pencils // LANES
    n_a = n_pen // 2
    assert n_a == groups and depth == 8 and nf == 5
    wides = pencils // WIDE
    n_hi = wides * depth
    p_bits, w_bits = log2(pencils), log2(WIDE)
    f32, i32 = jnp.float32, jnp.int32

    me_b = lax.axis_index("blk")
    me_p = lax.axis_index("pen")
    zh = lax.div(me_p, n_a)
    a = lax.rem(me_p, n_a)
    third = lax.rem(a, 2) == zh

    def lane_group(g):
        return pl.ds(pl.multiple_of(g * LANES, LANES), LANES)

    loads = {}
    for name, source, target in (
        ("owner", owner_hbm, owner_ref),
        ("state", state_hbm, state_ref),
        ("dcell", dcell_hbm, dcell_ref),
        ("dweight", dweight_hbm, dweight_ref),
        ("count", count_hbm, count_ref),
        ("rcell", rcell_hbm, rcell_ref),
        ("prev", prev_hbm, prev_ref),
        ("iblank", iblank_hbm, iblank_ref),
        ("speed", speed_hbm, speed_ref),
        ("left", left_hbm, left_ref),
        ("linv", linv_hbm, linv_ref),
        ("right", right_hbm, right_ref),
    ):
        loads[name] = pltpu.make_async_copy(source, target, load_sem.at[len(loads)])
        loads[name].start()

    def loaded(*names):
        for name in names:
            loads[name].wait()

    @pl.when(me_p == 0)
    def _():
        halo_in[0] = jnp.zeros(halo_in.shape[1:], f32)

    @pl.when(me_p == n_pen - 1)
    def _():
        halo_in[1] = jnp.zeros(halo_in.shape[1:], f32)

    barrier = pltpu.get_barrier_semaphore()

    def greet(where):
        pl.semaphore_signal(barrier, inc=1, device_id=where, device_id_type=MESH)
        return 0

    lax.fori_loop(1, n_blk, lambda off, _: greet({"blk": lax.rem(me_b + off, n_blk)}), 0)
    lax.fori_loop(1, n_pen, lambda off, _: greet({"pen": lax.rem(me_p + off, n_pen)}), 0)

    def met():
        pl.semaphore_wait(barrier, n_blk - 1 + n_pen - 1)

    lane = lax.broadcasted_iota(i32, (1, LANES), 1)
    lo_iota[...] = lax.broadcasted_iota(i32, (WIDE, LANES), 0).astype(f32).astype(jnp.bfloat16)

    def high_of(cells):
        wide = lax.shift_right_logical(cells, w_bits) & (wides - 1)
        return wide * depth + lax.shift_right_logical(cells, p_bits)

    def pick_lanes(cells):
        low = (cells & (WIDE - 1)).astype(f32).astype(jnp.bfloat16)
        return jnp.where(lo_iota[...] == low, jnp.bfloat16(1), jnp.bfloat16(0))

    loaded("owner")
    held = jnp.zeros((1, LANES), i32)
    for b in range(n_blk):
        held = jnp.where(lane == owner_ref[b], b, held)
    held_vec[...] = held
    held_copy = pltpu.make_async_copy(held_vec, held_ref, held_sem)
    held_copy.start()

    held_copy.wait()

    loaded("count", "state", "dcell", "dweight")
    tiles = [state_ref[m, :, w * WIDE : (w + 1) * WIDE] for m in range(nf) for w in range(wides)]
    n_rows = nf * n_hi
    parts[...] = jnp.concatenate(split(jnp.concatenate(tiles, axis=0)), axis=0)

    def fringe_offset(i):
        return n_blk // 2 + lax.div(i + 1, 2) * (2 * lax.rem(i, 2) - 1)

    def fringe_copy(slot, peer, source):
        return pltpu.make_async_remote_copy(
            src_ref=rows_out.at[slot],
            dst_ref=rows_in.at[source],
            send_sem=fringe_send.at[slot],
            recv_sem=fringe_recv.at[source],
            device_id={"blk": peer},
            device_id_type=MESH,
        )

    hi_iota = lax.broadcasted_iota(i32, (n_hi, LANES), 0)
    donors = dcell_ref.shape[1]

    across = lax.broadcasted_iota(i32, (LANES, WIDE), 1).astype(f32)

    def receivers(b):
        low = (rcell_ref[pl.ds(b, 1), :] & (WIDE - 1)).astype(f32)
        slots = jnp.broadcast_to(low, (LANES, LANES)).T
        slots = jnp.concatenate([slots] * (WIDE // LANES), axis=1)
        recv_lanes[b] = jnp.where(slots == across, 1.0, 0.0).astype(jnp.bfloat16)

    def interpolate(q, send, count):
        for u in range(TOGETHER):
            receivers(q * TOGETHER + u)
        for u in range(count):
            slot = q * TOGETHER + u
            peer = lax.rem(me_b + fringe_offset(slot), n_blk)
            block = held_ref[0, peer]
            cells, weights = dcell_ref[block], dweight_ref[block]
            acc = [None] * nf
            for i in range(0, donors, 2):
                pair = [cells[k : k + 1, :] for k in (i, i + 1)]
                picks = jnp.concatenate([pick_lanes(c) for c in pair], axis=1)
                both = jnp.dot(parts[...], picks, preferred_element_type=f32)
                both = both[:n_rows] + both[n_rows:]
                for k in range(2):
                    weight = jnp.where(hi_iota == high_of(pair[k]), weights[i + k : i + k + 1, :], 0.0)
                    for m in range(nf):
                        term = both[m * n_hi : (m + 1) * n_hi, k * LANES : (k + 1) * LANES] * weight
                        term = sum(term[w * depth : (w + 1) * depth] for w in range(wides))
                        acc[m] = term if acc[m] is None else acc[m] + term
            live = lane < count_ref[block]
            for m in range(nf):
                row = jnp.sum(acc[m], axis=0, keepdims=True)
                if m == 0:
                    row = jnp.where(live, row, DEAD)
                rows_out[slot, pl.ds(m, 1), :] = row

        if send:
            for u in range(count):
                send_ready(q * TOGETHER + u, 0)
        return 0

    def send_ready(slot, _):
        fringe_copy(slot, lax.rem(me_b + fringe_offset(slot), n_blk), me_b).start()
        return 0

    steps = n_blk // TOGETHER
    loaded("rcell")
    lax.fori_loop(0, steps // 2, lambda q, _: interpolate(q, False, TOGETHER), 0)
    met()
    lax.fori_loop(0, steps // 2 * TOGETHER, send_ready, 0)
    lax.fori_loop(steps // 2, steps - 1, lambda q, _: interpolate(q, True, TOGETHER), 0)
    interpolate(steps - 1, True, TOGETHER - 1)

    rows_in[me_b] = jnp.full(rows_in.shape[1:], DEAD, f32)

    placed[...] = jnp.zeros_like(placed)

    def place(q, _):
        sources = [lax.rem(me_b - fringe_offset(q * PLACED + u) + n_blk, n_blk) for u in range(PLACED)]
        for u in range(PLACED - 1):
            fringe_copy(q * PLACED + u, sources[u], sources[u]).wait_recv()
        last = q * PLACED + PLACED - 1

        @pl.when(last < n_blk - 1)
        def _():
            fringe_copy(last, sources[-1], sources[-1]).wait_recv()

        tall, flat = [], []
        for source in sources:
            block = held_ref[0, source]
            rows = [rows_in[source, m : m + 1, :] for m in range(nf)]
            here = (hi_iota == high_of(rcell_ref[pl.ds(block, 1), :])) & (rows[0] < 0.5 * DEAD)
            high, low = split(jnp.concatenate([jnp.where(here, row, 0.0) for row in rows], axis=0))
            hit = jnp.where(here, 1.0, 0.0).astype(jnp.bfloat16)
            tall.append(jnp.concatenate([high, low, hit], axis=0))
            flat.append(recv_lanes[block])
        placed[...] += jnp.dot(
            jnp.concatenate(tall, axis=1), jnp.concatenate(flat, axis=0), preferred_element_type=f32
        )
        return 0

    lax.fori_loop(0, n_blk // PLACED, place, 0)
    for m in range(nf):
        for w in range(wides):
            at, lanes = m * n_hi + w * depth, slice(w * WIDE, (w + 1) * WIDE)
            value = placed[at : at + depth, :] + placed[n_rows + at : n_rows + at + depth, :]
            hit = placed[2 * n_rows + w * depth : 2 * n_rows + (w + 1) * depth, :]
            filled[m, :, lanes] = jnp.where(hit > 0.5, value, state_ref[m, :, lanes])

    def halo_copy(way, peer):
        return pltpu.make_async_remote_copy(
            src_ref=halo_out.at[way],
            dst_ref=halo_in.at[way],
            send_sem=halo_send.at[way],
            recv_sem=halo_recv.at[way],
            device_id={"pen": peer},
            device_id_type=MESH,
        )

    halo_out[0] = filled[:, depth - 2 :, :]
    halo_out[1] = filled[:, :2, :]
    upward = halo_copy(0, lax.rem(me_p + 1, n_pen))
    downward = halo_copy(1, lax.rem(me_p + n_pen - 1, n_pen))

    @pl.when(me_p < n_pen - 1)
    def _():
        upward.start()

    @pl.when(me_p > 0)
    def _():
        downward.start()

    loaded("prev", "iblank", "speed", "left")
    layer = lax.broadcasted_iota(i32, (depth, pencils), 0)
    keep = iblank_ref[...].astype(f32)

    def wave(m):
        return jnp.concatenate([speed_ref[m * groups + g : m * groups + g + 1, :] for g in range(groups)], axis=1)

    for m in range(nf):
        cur = filled[m]
        upper = jnp.where(layer == depth - 1, 0.0, pltpu.roll(cur, depth - 1, 0))
        upper_two = jnp.where(layer >= depth - 2, 0.0, pltpu.roll(cur, depth - 2, 0))
        lower = jnp.where(layer == 0, 0.0, pltpu.roll(cur, 1, 0))
        lower_two = jnp.where(layer <= 1, 0.0, pltpu.roll(cur, 2, 0))
        r = -(cur - prev_ref[m]) - 0.5 * wave(m) * (upper - lower)
        r = r + 0.25 * (upper - 2.0 * cur + lower)
        r = r - 0.0625 * (upper_two - 4.0 * upper + 6.0 * cur - 4.0 * lower + lower_two)
        r = r - 0.25 * (pltpu.roll(cur, pencils - 1, 1) - pltpu.roll(cur, 1, 1))
        resid[m] = r * keep

    def mix(matrix_ref, value, m, g):
        total = None
        for n in range(nf):
            at = (m * nf + n) * groups + g
            term = matrix_ref[at : at + 1, :] * value(n, g)
            total = term if total is None else total + term
        return total

    def resid_at(n, g):
        return resid[n, :, g * LANES : (g + 1) * LANES]

    def place_of(m, g):
        return (g % 2, g, 2) if m == 4 else (m // 2, g, m % 2)

    def each_peer(do):
        lax.fori_loop(0, n_a, lambda i, _: do(1 - zh, lax.rem(a + i, n_a)), 0)
        lax.fori_loop(1, n_a, lambda i, _: do(zh, lax.rem(a + i, n_a)), 0)

    def each_source(do):
        lax.fori_loop(1, n_a, lambda i, _: do(zh, lax.rem(a + n_a - i, n_a)), 0)
        lax.fori_loop(0, n_a, lambda i, _: do(1 - zh, lax.rem(a + n_a - i, n_a)), 0)

    def takes_third(half, g):
        return lax.rem(g, 2) == half

    MESSAGES = ((0, 0, 2), (1, 0, 1), (1, 1, 1))
    ANSWERS = ((0, 1), (1, 1))

    def sized(first, count, more, do):
        if first + count < 2:
            do(count)
            return 0

        @pl.when(more)
        def _():
            do(count + 1)

        @pl.when(jnp.logical_not(more))
        def _():
            do(count)

        return 0

    def fwd_copy(message, half, g, source, count):
        part, first, _ = MESSAGES[message]
        peer = half * n_a + g
        return pltpu.make_async_remote_copy(
            src_ref=work.at[part, half, g, pl.ds(first, count)],
            dst_ref=parts_in.at[part, source, pl.ds(first, count)],
            send_sem=fwd_send.at[message, peer],
            recv_sem=fwd_recv.at[message, source],
            device_id={"pen": peer},
            device_id_type=MESH,
        )

    def send_message(message):
        part, first, count = MESSAGES[message]
        each_peer(
            lambda half, g: sized(
                first, count, takes_third(half, g), lambda n: fwd_copy(message, half, g, me_p, n).start()
            )
        )

        def keep_own(n):
            parts_in[part, me_p, first : first + n] = work[part, zh, a, first : first + n]

        sized(first, count, third, keep_own)

    for g in range(groups):
        for m in range(nf):
            work[(0, *place_of(m, g))] = mix(left_ref, resid_at, m, g)[2 : depth - 2, :]
    send_message(0)

    @pl.when(me_p > 0)
    def _():
        upward.wait_recv()

    @pl.when(me_p < n_pen - 1)
    def _():
        downward.wait_recv()

    for m in range(nf):
        low2, low1 = halo_in[0, m, 0:1, :], halo_in[0, m, 1:2, :]
        up1, up2 = halo_in[1, m, 0:1, :], halo_in[1, m, 1:2, :]
        speed = wave(m)
        first = (0.5 + 0.5 * speed) * low1 - 0.0625 * low2
        last = (0.5 - 0.5 * speed) * up1 - 0.0625 * up2
        second, last_but = -0.0625 * low1, -0.0625 * up1
        extra = jnp.where(
            layer == 0,
            first,
            jnp.where(layer == 1, second, jnp.where(layer == depth - 1, last, jnp.where(layer == depth - 2, last_but, 0.0))),
        )
        resid[m] = resid[m] + extra * keep

    for g in range(groups):
        for m in range(nf):
            half, at, f = place_of(m, g)
            mixed = mix(left_ref, resid_at, m, g)
            work[1, half, at, f, 0:2, :] = mixed[0:2, :]
            work[1, half, at, f, 2:4, :] = mixed[depth - 2 :, :]
    send_message(1)
    send_message(2)

    def fringe_left(i, _):
        fringe_copy(i, me_b, me_b).wait_send()
        return 0

    lax.fori_loop(0, n_blk - 1, fringe_left, 0)

    @pl.when(me_p < n_pen - 1)
    def _():
        upward.wait_send()

    @pl.when(me_p > 0)
    def _():
        downward.wait_send()

    loaded("linv", "right")
    def await_message(message):
        _, first, count = MESSAGES[message]
        each_source(
            lambda half, g: sized(
                first, count, third, lambda n: fwd_copy(message, half, g, half * n_a + g, n).wait_recv()
            )
        )

    def solve(f):
        for p in range(n_pen):
            work_line[p * depth : p * depth + 2, :] = parts_in[1, p, f, 0:2, :]
            work_line[p * depth + 2 : p * depth + 6, :] = parts_in[0, p, f]
            work_line[p * depth + 6 : (p + 1) * depth, :] = parts_in[1, p, f, 2:4, :]
        inv_high, inv_low = split(linv_ref[4 if f == 2 else zh * 2 + f])
        line_high, line_low = split(work_line[...])
        line = jnp.dot(
            jnp.concatenate([inv_high, inv_high, inv_low], axis=1),
            jnp.concatenate([line_high, line_low, line_high], axis=0),
            preferred_element_type=f32,
        )
        for p in range(n_pen):
            solved_line[p, f] = line[p * depth : (p + 1) * depth, :]

    def back_copy(answer, peer, half, g, count):
        first = ANSWERS[answer][0]
        return pltpu.make_async_remote_copy(
            src_ref=solved_line.at[peer, pl.ds(first, count)],
            dst_ref=solved.at[half, g, pl.ds(first, count)],
            send_sem=back_send.at[answer, peer],
            recv_sem=back_recv.at[answer, half * n_a + g],
            device_id={"pen": peer},
            device_id_type=MESH,
        )

    def send_answer(answer):
        first, count = ANSWERS[answer]
        each_peer(
            lambda half, g: sized(
                first, count, third, lambda n: back_copy(answer, half * n_a + g, zh, a, n).start()
            )
        )

        def keep_solved(n):
            solved[zh, a, first : first + n] = solved_line[me_p, first : first + n]

        sized(first, count, third, keep_solved)

    await_message(0)
    await_message(1)
    solve(0)
    send_answer(0)
    await_message(2)
    solve(1)

    @pl.when(third)
    def _():
        solve(2)

    send_answer(1)

    def left(half, g):
        for message, (_, first, count) in enumerate(MESSAGES):
            sized(first, count, takes_third(half, g), lambda n: fwd_copy(message, half, g, me_p, n).wait_send())
        for answer, (first, count) in enumerate(ANSWERS):
            sized(first, count, third, lambda n: back_copy(answer, half * n_a + g, zh, a, n).wait_send())
        return 0

    each_peer(left)

    def answered(half, g):
        for answer, (first, count) in enumerate(ANSWERS):
            sized(
                first, count, takes_third(half, g), lambda n: back_copy(answer, half * n_a + g, half, g, n).wait_recv()
            )
        return 0

    each_source(answered)

    def solved_at(n, g):
        return solved[place_of(n, g)]

    for g in range(groups):
        lanes = slice(g * LANES, (g + 1) * LANES)
        for m in range(nf):
            out_ref[m, :, lanes] = filled[m, :, lanes] + keep[:, lanes] * mix(right_ref, solved_at, m, g)


def solution(mesh):
    n_blk, n_pen = mesh.shape["blk"], mesh.shape["pen"]

    def shards(
        state,
        previous,
        iblank,
        block_owner,
        donor_cell,
        donor_weight,
        send_count,
        recv_cell,
        speed,
        left_vectors,
        right_vectors,
        line_inverse,
    ):
        _, depth, nf, pencils = state.shape
        groups, n_hi = pencils // LANES, pencils // WIDE * depth
        points = line_inverse.shape[-1]
        cap, donors = recv_cell.shape[-1], donor_cell.shape[-1]
        f32 = jnp.float32
        hbm = pl.BlockSpec(memory_space=pltpu.HBM)
        vmem = pl.BlockSpec(memory_space=pltpu.VMEM)
        dma = pltpu.SemaphoreType.DMA
        out = pl.pallas_call(
            functools.partial(kernel, n_blk, n_pen),
            out_shape=jax.ShapeDtypeStruct((nf, depth, pencils), f32),
            in_specs=[hbm] * 12,
            out_specs=vmem,
            scratch_shapes=[
                pltpu.SMEM((n_blk,), jnp.int32),
                pltpu.SMEM((n_blk,), jnp.int32),
                pltpu.VMEM((nf, depth, pencils), f32),
                pltpu.VMEM((nf, depth, pencils), f32),
                pltpu.VMEM((depth, pencils), jnp.int32),
                pltpu.VMEM((n_blk, donors, cap), jnp.int32),
                pltpu.VMEM((n_blk, donors, cap), f32),
                pltpu.VMEM((n_blk, cap), jnp.int32),
                pltpu.VMEM((nf * groups, LANES), f32),
                pltpu.VMEM((nf * nf * groups, LANES), f32),
                pltpu.VMEM((nf * nf * groups, LANES), f32),
                pltpu.VMEM((nf, points, points), f32),
                dma((12,)),
                pltpu.VMEM((1, LANES), jnp.int32),
                pltpu.SMEM((1, LANES), jnp.int32),
                dma(()),
                pltpu.VMEM((WIDE, LANES), jnp.bfloat16),
                pltpu.VMEM((n_blk, LANES, WIDE), jnp.bfloat16),
                pltpu.VMEM((2 * nf * n_hi, WIDE), jnp.bfloat16),
                pltpu.VMEM(((2 * nf + 1) * n_hi, WIDE), f32),
                pltpu.VMEM((n_blk, nf, cap), f32),
                pltpu.VMEM((n_blk, nf, cap), f32),
                pltpu.VMEM((nf, depth, pencils), f32),
                pltpu.VMEM((2, nf, 2, pencils), f32),
                pltpu.VMEM((2, nf, 2, pencils), f32),
                pltpu.VMEM((nf, depth, pencils), f32),
                pltpu.VMEM((2, 2, groups, 3, depth // 2, LANES), f32),
                pltpu.VMEM((2, n_pen, 3, depth // 2, LANES), f32),
                pltpu.VMEM((points, LANES), f32),
                pltpu.VMEM((n_pen, 3, depth, LANES), f32),
                pltpu.VMEM((2, groups, 3, depth, LANES), f32),
                dma((n_blk,)),
                dma((n_blk,)),
                dma((2,)),
                dma((2,)),
                dma((3, n_pen)),
                dma((3, n_pen)),
                dma((2, n_pen)),
                dma((2, n_pen)),
            ],
            compiler_params=pltpu.CompilerParams(
                collective_id=0, has_side_effects=True, vmem_limit_bytes=60 * 1024 * 1024
            ),
        )(
            block_owner,
            send_count.reshape(n_blk),
            state[0].transpose(1, 0, 2),
            previous[0].transpose(1, 0, 2),
            iblank[0],
            donor_cell[0, 0].transpose(0, 2, 1),
            donor_weight[0, 0].transpose(0, 2, 1),
            recv_cell[0, 0],
            speed.reshape(nf * groups, LANES),
            left_vectors.reshape(nf * nf * groups, LANES),
            right_vectors.reshape(nf * nf * groups, LANES),
            line_inverse[0],
        )
        return out.transpose(1, 0, 2)[None]

    placed = (
        P("blk", "pen", None, None),
        P("blk", "pen", None, None),
        P("blk", "pen", None),
        P(),
        P("pen", "blk", None, None, None),
        P("pen", "blk", None, None, None),
        P("pen", "blk", None),
        P("pen", "blk", None, None),
        P("blk", None, None),
        P("blk", None, None, None),
        P("blk", None, None, None),
        P("blk", None, None, None),
    )
    return jax.shard_map(
        shards, mesh=mesh, in_specs=placed, out_specs=P("blk", "pen", None, None), check_vma=False
    )
```

```python
import functools

import jax
import jax.numpy as jnp
from jax import lax
from jax.experimental import pallas as pl
from jax.experimental.pallas import tpu as pltpu
from jax.sharding import PartitionSpec as P

MESH = pl.DeviceIdType.MESH
LANES = 128
DEAD = 1e30
WIDE = 256
TOGETHER = 8
PLACED = 4


def split(value):
    high = value.astype(jnp.bfloat16)
    return high, (value - high.astype(jnp.float32)).astype(jnp.bfloat16)


def log2(n):
    assert n & (n - 1) == 0
    return n.bit_length() - 1


def kernel(
    n_blk,
    n_pen,
    owner_hbm,
    count_hbm,
    state_hbm,
    prev_hbm,
    iblank_hbm,
    dcell_hbm,
    dweight_hbm,
    rcell_hbm,
    speed_hbm,
    left_hbm,
    right_hbm,
    linv_hbm,
    out_ref,
    owner_ref,
    count_ref,
    state_ref,
    prev_ref,
    iblank_ref,
    dcell_ref,
    dweight_ref,
    rcell_ref,
    speed_ref,
    left_ref,
    right_ref,
    linv_ref,
    load_sem,
    held_vec,
    held_ref,
    held_sem,
    lo_iota,
    recv_lanes,
    parts,
    placed,
    rows_out,
    rows_in,
    filled,
    halo_out,
    halo_in,
    resid,
    work,
    parts_in,
    work_line,
    solved_line,
    solved,
    fringe_send,
    fringe_recv,
    halo_send,
    halo_recv,
    fwd_send,
    fwd_recv,
    back_send,
    back_recv,
):
    nf, depth, pencils = state_hbm.shape
    groups = pencils // LANES
    n_a = n_pen // 2
    assert n_a == groups and depth == 8 and nf == 5
    wides = pencils // WIDE
    n_hi = wides * depth
    p_bits, w_bits = log2(pencils), log2(WIDE)
    f32, i32 = jnp.float32, jnp.int32

    me_b = lax.axis_index("blk")
    me_p = lax.axis_index("pen")
    zh = lax.div(me_p, n_a)
    a = lax.rem(me_p, n_a)
    third = lax.rem(a, 2) == zh

    def lane_group(g):
        return pl.ds(pl.multiple_of(g * LANES, LANES), LANES)

    loads = {}
    for name, source, target in (
        ("owner", owner_hbm, owner_ref),
        ("state", state_hbm, state_ref),
        ("dcell", dcell_hbm, dcell_ref),
        ("dweight", dweight_hbm, dweight_ref),
        ("count", count_hbm, count_ref),
        ("rcell", rcell_hbm, rcell_ref),
        ("prev", prev_hbm, prev_ref),
        ("iblank", iblank_hbm, iblank_ref),
        ("speed", speed_hbm, speed_ref),
        ("left", left_hbm, left_ref),
        ("linv", linv_hbm, linv_ref),
        ("right", right_hbm, right_ref),
    ):
        loads[name] = pltpu.make_async_copy(source, target, load_sem.at[len(loads)])
        loads[name].start()

    def loaded(*names):
        for name in names:
            loads[name].wait()

    @pl.when(me_p == 0)
    def _():
        halo_in[0] = jnp.zeros(halo_in.shape[1:], f32)

    @pl.when(me_p == n_pen - 1)
    def _():
        halo_in[1] = jnp.zeros(halo_in.shape[1:], f32)

    barrier = pltpu.get_barrier_semaphore()

    def greet(where):
        pl.semaphore_signal(barrier, inc=1, device_id=where, device_id_type=MESH)
        return 0

    lax.fori_loop(1, n_blk, lambda off, _: greet({"blk": lax.rem(me_b + off, n_blk)}), 0)
    lax.fori_loop(1, n_pen, lambda off, _: greet({"pen": lax.rem(me_p + off, n_pen)}), 0)

    def met():
        pl.semaphore_wait(barrier, n_blk - 1 + n_pen - 1)

    lane = lax.broadcasted_iota(i32, (1, LANES), 1)
    lo_iota[...] = lax.broadcasted_iota(i32, (WIDE, LANES), 0).astype(f32).astype(jnp.bfloat16)

    def high_of(cells):
        wide = lax.shift_right_logical(cells, w_bits) & (wides - 1)
        return wide * depth + lax.shift_right_logical(cells, p_bits)

    def pick_lanes(cells):
        low = (cells & (WIDE - 1)).astype(f32).astype(jnp.bfloat16)
        return jnp.where(lo_iota[...] == low, jnp.bfloat16(1), jnp.bfloat16(0))

    loaded("owner")
    held = jnp.zeros((1, LANES), i32)
    for b in range(n_blk):
        held = jnp.where(lane == owner_ref[b], b, held)
    held_vec[...] = held
    held_copy = pltpu.make_async_copy(held_vec, held_ref, held_sem)
    held_copy.start()

    held_copy.wait()

    loaded("count", "state", "dcell", "dweight")
    tiles = [state_ref[m, :, w * WIDE : (w + 1) * WIDE] for m in range(nf) for w in range(wides)]
    n_rows = nf * n_hi
    parts[...] = jnp.concatenate(split(jnp.concatenate(tiles, axis=0)), axis=0)

    def fringe_offset(i):
        return n_blk // 2 + lax.div(i + 1, 2) * (2 * lax.rem(i, 2) - 1)

    def fringe_copy(slot, peer, source):
        return pltpu.make_async_remote_copy(
            src_ref=rows_out.at[slot],
            dst_ref=rows_in.at[source],
            send_sem=fringe_send.at[slot],
            recv_sem=fringe_recv.at[source],
            device_id={"blk": peer},
            device_id_type=MESH,
        )

    hi_iota = lax.broadcasted_iota(i32, (n_hi, LANES), 0)
    donors = dcell_ref.shape[1]

    across = lax.broadcasted_iota(i32, (LANES, WIDE), 1).astype(f32)

    def receivers(b):
        low = (rcell_ref[pl.ds(b, 1), :] & (WIDE - 1)).astype(f32)
        slots = jnp.broadcast_to(low, (LANES, LANES)).T
        slots = jnp.concatenate([slots] * (WIDE // LANES), axis=1)
        recv_lanes[b] = jnp.where(slots == across, 1.0, 0.0).astype(jnp.bfloat16)

    def send_ready(slot, _):
        fringe_copy(slot, lax.rem(me_b + fringe_offset(slot), n_blk), me_b).start()
        return 0

    together = min(TOGETHER, n_blk)
    steps = n_blk // together

    def interpolate(q, _):
        @pl.when(q == steps // 2)
        def _():
            met()
            lax.fori_loop(0, steps // 2 * together, send_ready, 0)

        for u in range(together):
            receivers(q * together + u)
        for u in range(together):
            slot = q * together + u
            peer = lax.rem(me_b + fringe_offset(slot), n_blk)
            block = held_ref[0, peer]
            cells, weights = dcell_ref[block], dweight_ref[block]
            acc = [None] * nf
            for i in range(0, donors, 2):
                pair = [cells[k : k + 1, :] for k in (i, i + 1)]
                picks = jnp.concatenate([pick_lanes(c) for c in pair], axis=1)
                both = jnp.dot(parts[...], picks, preferred_element_type=f32)
                both = both[:n_rows] + both[n_rows:]
                for k in range(2):
                    weight = jnp.where(hi_iota == high_of(pair[k]), weights[i + k : i + k + 1, :], 0.0)
                    for m in range(nf):
                        term = both[m * n_hi : (m + 1) * n_hi, k * LANES : (k + 1) * LANES] * weight
                        term = sum(term[w * depth : (w + 1) * depth] for w in range(wides))
                        acc[m] = term if acc[m] is None else acc[m] + term
            live = lane < count_ref[block]
            for m in range(nf):
                row = jnp.sum(acc[m], axis=0, keepdims=True)
                if m == 0:
                    row = jnp.where(live, row, DEAD)
                rows_out[slot, pl.ds(m, 1), :] = row

        @pl.when(q >= steps // 2)
        def _():
            for u in range(together - 1):
                send_ready(q * together + u, 0)

            @pl.when(q < steps - 1)
            def _():
                send_ready(q * together + together - 1, 0)

        return 0

    loaded("rcell")
    lax.fori_loop(0, steps, interpolate, 0)
    rows_in[me_b] = jnp.full(rows_in.shape[1:], DEAD, f32)

    placed[...] = jnp.zeros_like(placed)

    def place(q, _):
        sources = [lax.rem(me_b - fringe_offset(q * PLACED + u) + n_blk, n_blk) for u in range(PLACED)]
        for u in range(PLACED - 1):
            fringe_copy(q * PLACED + u, sources[u], sources[u]).wait_recv()
        last = q * PLACED + PLACED - 1

        @pl.when(last < n_blk - 1)
        def _():
            fringe_copy(last, sources[-1], sources[-1]).wait_recv()

        tall, flat = [], []
        for source in sources:
            block = held_ref[0, source]
            rows = [rows_in[source, m : m + 1, :] for m in range(nf)]
            here = (hi_iota == high_of(rcell_ref[pl.ds(block, 1), :])) & (rows[0] < 0.5 * DEAD)
            high, low = split(jnp.concatenate([jnp.where(here, row, 0.0) for row in rows], axis=0))
            hit = jnp.where(here, 1.0, 0.0).astype(jnp.bfloat16)
            tall.append(jnp.concatenate([high, low, hit], axis=0))
            flat.append(recv_lanes[block])
        placed[...] += jnp.dot(
            jnp.concatenate(tall, axis=1), jnp.concatenate(flat, axis=0), preferred_element_type=f32
        )
        return 0

    lax.fori_loop(0, n_blk // PLACED, place, 0)
    for m in range(nf):
        for w in range(wides):
            at, lanes = m * n_hi + w * depth, slice(w * WIDE, (w + 1) * WIDE)
            value = placed[at : at + depth, :] + placed[n_rows + at : n_rows + at + depth, :]
            hit = placed[2 * n_rows + w * depth : 2 * n_rows + (w + 1) * depth, :]
            filled[m, :, lanes] = jnp.where(hit > 0.5, value, state_ref[m, :, lanes])

    def halo_copy(way, peer):
        return pltpu.make_async_remote_copy(
            src_ref=halo_out.at[way],
            dst_ref=halo_in.at[way],
            send_sem=halo_send.at[way],
            recv_sem=halo_recv.at[way],
            device_id={"pen": peer},
            device_id_type=MESH,
        )

    halo_out[0] = filled[:, depth - 2 :, :]
    halo_out[1] = filled[:, :2, :]
    upward = halo_copy(0, lax.rem(me_p + 1, n_pen))
    downward = halo_copy(1, lax.rem(me_p + n_pen - 1, n_pen))

    @pl.when(me_p < n_pen - 1)
    def _():
        upward.start()

    @pl.when(me_p > 0)
    def _():
        downward.start()

    loaded("prev", "iblank", "speed", "left")
    layer = lax.broadcasted_iota(i32, (depth, pencils), 0)
    keep = iblank_ref[...].astype(f32)

    def wave(m):
        return jnp.concatenate([speed_ref[m * groups + g : m * groups + g + 1, :] for g in range(groups)], axis=1)

    for m in range(nf):
        cur = filled[m]
        upper = jnp.where(layer == depth - 1, 0.0, pltpu.roll(cur, depth - 1, 0))
        upper_two = jnp.where(layer >= depth - 2, 0.0, pltpu.roll(cur, depth - 2, 0))
        lower = jnp.where(layer == 0, 0.0, pltpu.roll(cur, 1, 0))
        lower_two = jnp.where(layer <= 1, 0.0, pltpu.roll(cur, 2, 0))
        r = -(cur - prev_ref[m]) - 0.5 * wave(m) * (upper - lower)
        r = r + 0.25 * (upper - 2.0 * cur + lower)
        r = r - 0.0625 * (upper_two - 4.0 * upper + 6.0 * cur - 4.0 * lower + lower_two)
        r = r - 0.25 * (pltpu.roll(cur, pencils - 1, 1) - pltpu.roll(cur, 1, 1))
        resid[m] = r * keep

    def mix(matrix_ref, value, m, g):
        total = None
        for n in range(nf):
            at = (m * nf + n) * groups + g
            term = matrix_ref[at : at + 1, :] * value(n, g)
            total = term if total is None else total + term
        return total

    def resid_at(n, g):
        return resid[n, :, g * LANES : (g + 1) * LANES]

    def place_of(m, g):
        return (g % 2, g, 2) if m == 4 else (m // 2, g, m % 2)

    def each_peer(do):
        lax.fori_loop(0, n_a, lambda i, _: do(1 - zh, lax.rem(a + i, n_a)), 0)
        lax.fori_loop(1, n_a, lambda i, _: do(zh, lax.rem(a + i, n_a)), 0)

    def each_source(do):
        lax.fori_loop(1, n_a, lambda i, _: do(zh, lax.rem(a + n_a - i, n_a)), 0)
        lax.fori_loop(0, n_a, lambda i, _: do(1 - zh, lax.rem(a + n_a - i, n_a)), 0)

    def takes_third(half, g):
        return lax.rem(g, 2) == half

    MESSAGES = ((0, 0, 2), (1, 0, 2))
    ANSWERS = ((0, 2),)

    def sized(first, count, more, do):
        if first + count < 2:
            do(count)
            return 0

        @pl.when(more)
        def _():
            do(count + 1)

        @pl.when(jnp.logical_not(more))
        def _():
            do(count)

        return 0

    def fwd_copy(message, half, g, source, count):
        part, first, _ = MESSAGES[message]
        peer = half * n_a + g
        return pltpu.make_async_remote_copy(
            src_ref=work.at[part, half, g, pl.ds(first, count)],
            dst_ref=parts_in.at[part, source, pl.ds(first, count)],
            send_sem=fwd_send.at[message, peer],
            recv_sem=fwd_recv.at[message, source],
            device_id={"pen": peer},
            device_id_type=MESH,
        )

    def send_message(message):
        part, first, count = MESSAGES[message]
        each_peer(
            lambda half, g: sized(
                first, count, takes_third(half, g), lambda n: fwd_copy(message, half, g, me_p, n).start()
            )
        )

        def keep_own(n):
            parts_in[part, me_p, first : first + n] = work[part, zh, a, first : first + n]

        sized(first, count, third, keep_own)

    for g in range(groups):
        for m in range(nf):
            work[(0, *place_of(m, g))] = mix(left_ref, resid_at, m, g)[2 : depth - 2, :]
    send_message(0)

    @pl.when(me_p > 0)
    def _():
        upward.wait_recv()

    @pl.when(me_p < n_pen - 1)
    def _():
        downward.wait_recv()

    for m in range(nf):
        low2, low1 = halo_in[0, m, 0:1, :], halo_in[0, m, 1:2, :]
        up1, up2 = halo_in[1, m, 0:1, :], halo_in[1, m, 1:2, :]
        speed = wave(m)
        first = (0.5 + 0.5 * speed) * low1 - 0.0625 * low2
        last = (0.5 - 0.5 * speed) * up1 - 0.0625 * up2
        second, last_but = -0.0625 * low1, -0.0625 * up1
        extra = jnp.where(
            layer == 0,
            first,
            jnp.where(layer == 1, second, jnp.where(layer == depth - 1, last, jnp.where(layer == depth - 2, last_but, 0.0))),
        )
        resid[m] = resid[m] + extra * keep

    for g in range(groups):
        for m in range(nf):
            half, at, f = place_of(m, g)
            mixed = mix(left_ref, resid_at, m, g)
            work[1, half, at, f, 0:2, :] = mixed[0:2, :]
            work[1, half, at, f, 2:4, :] = mixed[depth - 2 :, :]
    send_message(1)

    def fringe_left(i, _):
        fringe_copy(i, me_b, me_b).wait_send()
        return 0

    lax.fori_loop(0, n_blk - 1, fringe_left, 0)

    @pl.when(me_p < n_pen - 1)
    def _():
        upward.wait_send()

    @pl.when(me_p > 0)
    def _():
        downward.wait_send()

    loaded("linv", "right")
    def await_message(message):
        _, first, count = MESSAGES[message]
        each_source(
            lambda half, g: sized(
                first, count, third, lambda n: fwd_copy(message, half, g, half * n_a + g, n).wait_recv()
            )
        )

    def solve(f):
        for p in range(n_pen):
            work_line[p * depth : p * depth + 2, :] = parts_in[1, p, f, 0:2, :]
            work_line[p * depth + 2 : p * depth + 6, :] = parts_in[0, p, f]
            work_line[p * depth + 6 : (p + 1) * depth, :] = parts_in[1, p, f, 2:4, :]
        inv_high, inv_low = split(linv_ref[4 if f == 2 else zh * 2 + f])
        line_high, line_low = split(work_line[...])
        line = jnp.dot(
            jnp.concatenate([inv_high, inv_high, inv_low], axis=1),
            jnp.concatenate([line_high, line_low, line_high], axis=0),
            preferred_element_type=f32,
        )
        for p in range(n_pen):
            solved_line[p, f] = line[p * depth : (p + 1) * depth, :]

    def back_copy(answer, peer, half, g, count):
        first = ANSWERS[answer][0]
        return pltpu.make_async_remote_copy(
            src_ref=solved_line.at[peer, pl.ds(first, count)],
            dst_ref=solved.at[half, g, pl.ds(first, count)],
            send_sem=back_send.at[answer, peer],
            recv_sem=back_recv.at[answer, half * n_a + g],
            device_id={"pen": peer},
            device_id_type=MESH,
        )

    def send_answer(answer):
        first, count = ANSWERS[answer]
        each_peer(
            lambda half, g: sized(
                first, count, third, lambda n: back_copy(answer, half * n_a + g, zh, a, n).start()
            )
        )

        def keep_solved(n):
            solved[zh, a, first : first + n] = solved_line[me_p, first : first + n]

        sized(first, count, third, keep_solved)

    await_message(0)
    await_message(1)
    solve(0)
    solve(1)

    @pl.when(third)
    def _():
        solve(2)

    send_answer(0)

    def left(half, g):
        for message, (_, first, count) in enumerate(MESSAGES):
            sized(first, count, takes_third(half, g), lambda n: fwd_copy(message, half, g, me_p, n).wait_send())
        for answer, (first, count) in enumerate(ANSWERS):
            sized(first, count, third, lambda n: back_copy(answer, half * n_a + g, zh, a, n).wait_send())
        return 0

    each_peer(left)

    def answered(half, g):
        for answer, (first, count) in enumerate(ANSWERS):
            sized(
                first, count, takes_third(half, g), lambda n: back_copy(answer, half * n_a + g, half, g, n).wait_recv()
            )
        return 0

    each_source(answered)

    def solved_at(n, g):
        return solved[place_of(n, g)]

    for g in range(groups):
        lanes = slice(g * LANES, (g + 1) * LANES)
        for m in range(nf):
            out_ref[m, :, lanes] = filled[m, :, lanes] + keep[:, lanes] * mix(right_ref, solved_at, m, g)


def solution(mesh):
    n_blk, n_pen = mesh.shape["blk"], mesh.shape["pen"]

    def shards(
        state,
        previous,
        iblank,
        block_owner,
        donor_cell,
        donor_weight,
        send_count,
        recv_cell,
        speed,
        left_vectors,
        right_vectors,
        line_inverse,
    ):
        _, depth, nf, pencils = state.shape
        groups, n_hi = pencils // LANES, pencils // WIDE * depth
        points = line_inverse.shape[-1]
        cap, donors = recv_cell.shape[-1], donor_cell.shape[-1]
        f32 = jnp.float32
        hbm = pl.BlockSpec(memory_space=pltpu.HBM)
        vmem = pl.BlockSpec(memory_space=pltpu.VMEM)
        dma = pltpu.SemaphoreType.DMA
        out = pl.pallas_call(
            functools.partial(kernel, n_blk, n_pen),
            out_shape=jax.ShapeDtypeStruct((nf, depth, pencils), f32),
            in_specs=[hbm] * 12,
            out_specs=vmem,
            scratch_shapes=[
                pltpu.SMEM((n_blk,), jnp.int32),
                pltpu.SMEM((n_blk,), jnp.int32),
                pltpu.VMEM((nf, depth, pencils), f32),
                pltpu.VMEM((nf, depth, pencils), f32),
                pltpu.VMEM((depth, pencils), jnp.int32),
                pltpu.VMEM((n_blk, donors, cap), jnp.int32),
                pltpu.VMEM((n_blk, donors, cap), f32),
                pltpu.VMEM((n_blk, cap), jnp.int32),
                pltpu.VMEM((nf * groups, LANES), f32),
                pltpu.VMEM((nf * nf * groups, LANES), f32),
                pltpu.VMEM((nf * nf * groups, LANES), f32),
                pltpu.VMEM((nf, points, points), f32),
                dma((12,)),
                pltpu.VMEM((1, LANES), jnp.int32),
                pltpu.SMEM((1, LANES), jnp.int32),
                dma(()),
                pltpu.VMEM((WIDE, LANES), jnp.bfloat16),
                pltpu.VMEM((n_blk, LANES, WIDE), jnp.bfloat16),
                pltpu.VMEM((2 * nf * n_hi, WIDE), jnp.bfloat16),
                pltpu.VMEM(((2 * nf + 1) * n_hi, WIDE), f32),
                pltpu.VMEM((n_blk, nf, cap), f32),
                pltpu.VMEM((n_blk, nf, cap), f32),
                pltpu.VMEM((nf, depth, pencils), f32),
                pltpu.VMEM((2, nf, 2, pencils), f32),
                pltpu.VMEM((2, nf, 2, pencils), f32),
                pltpu.VMEM((nf, depth, pencils), f32),
                pltpu.VMEM((2, 2, groups, 3, depth // 2, LANES), f32),
                pltpu.VMEM((2, n_pen, 3, depth // 2, LANES), f32),
                pltpu.VMEM((points, LANES), f32),
                pltpu.VMEM((n_pen, 3, depth, LANES), f32),
                pltpu.VMEM((2, groups, 3, depth, LANES), f32),
                dma((n_blk,)),
                dma((n_blk,)),
                dma((2,)),
                dma((2,)),
                dma((2, n_pen)),
                dma((2, n_pen)),
                dma((1, n_pen)),
                dma((1, n_pen)),
            ],
            compiler_params=pltpu.CompilerParams(
                collective_id=0, has_side_effects=True, vmem_limit_bytes=60 * 1024 * 1024
            ),
        )(
            block_owner,
            send_count.reshape(n_blk),
            state[0].transpose(1, 0, 2),
            previous[0].transpose(1, 0, 2),
            iblank[0],
            donor_cell[0, 0].transpose(0, 2, 1),
            donor_weight[0, 0].transpose(0, 2, 1),
            recv_cell[0, 0],
            speed.reshape(nf * groups, LANES),
            left_vectors.reshape(nf * nf * groups, LANES),
            right_vectors.reshape(nf * nf * groups, LANES),
            line_inverse[0],
        )
        return out.transpose(1, 0, 2)[None]

    placed = (
        P("blk", "pen", None, None),
        P("blk", "pen", None, None),
        P("blk", "pen", None),
        P(),
        P("pen", "blk", None, None, None),
        P("pen", "blk", None, None, None),
        P("pen", "blk", None),
        P("pen", "blk", None, None),
        P("blk", None, None),
        P("blk", None, None, None),
        P("blk", None, None, None),
        P("blk", None, None, None),
    )
    return jax.shard_map(
        shards, mesh=mesh, in_specs=placed, out_specs=P("blk", "pen", None, None), check_vma=False
    )
```

```python
import functools

import jax
import jax.numpy as jnp
from jax import lax
from jax.experimental import pallas as pl
from jax.experimental.pallas import tpu as pltpu
from jax.sharding import PartitionSpec as P

MESH = pl.DeviceIdType.MESH
LANES = 128
DEAD = 1e30
WIDE = 256
TOGETHER = 8
PLACED = 8


def split(value):
    high = value.astype(jnp.bfloat16)
    return high, (value - high.astype(jnp.float32)).astype(jnp.bfloat16)


def log2(n):
    assert n & (n - 1) == 0
    return n.bit_length() - 1


def kernel(
    n_blk,
    n_pen,
    owner_hbm,
    count_hbm,
    state_hbm,
    prev_hbm,
    iblank_hbm,
    dcell_hbm,
    dweight_hbm,
    rcell_hbm,
    speed_hbm,
    left_hbm,
    right_hbm,
    linv_hbm,
    out_ref,
    owner_ref,
    count_ref,
    state_ref,
    prev_ref,
    iblank_ref,
    dcell_ref,
    dweight_ref,
    rcell_ref,
    speed_ref,
    left_ref,
    right_ref,
    linv_ref,
    load_sem,
    held_vec,
    held_ref,
    held_sem,
    lo_iota,
    recv_lanes,
    parts,
    placed,
    rows_out,
    rows_in,
    filled,
    halo_out,
    halo_in,
    resid,
    work,
    parts_in,
    work_line,
    solved_line,
    solved,
    fringe_send,
    fringe_recv,
    halo_send,
    halo_recv,
    fwd_send,
    fwd_recv,
    back_send,
    back_recv,
):
    nf, depth, pencils = state_hbm.shape
    groups = pencils // LANES
    n_a = n_pen // 2
    assert n_a == groups and depth == 8 and nf == 5
    wides = pencils // WIDE
    n_hi = wides * depth
    p_bits, w_bits = log2(pencils), log2(WIDE)
    f32, i32 = jnp.float32, jnp.int32

    me_b = lax.axis_index("blk")
    me_p = lax.axis_index("pen")
    zh = lax.div(me_p, n_a)
    a = lax.rem(me_p, n_a)
    third = lax.rem(a, 2) == zh

    def lane_group(g):
        return pl.ds(pl.multiple_of(g * LANES, LANES), LANES)

    loads = {}
    for name, source, target in (
        ("owner", owner_hbm, owner_ref),
        ("state", state_hbm, state_ref),
        ("dcell", dcell_hbm, dcell_ref),
        ("dweight", dweight_hbm, dweight_ref),
        ("count", count_hbm, count_ref),
        ("rcell", rcell_hbm, rcell_ref),
        ("prev", prev_hbm, prev_ref),
        ("iblank", iblank_hbm, iblank_ref),
        ("speed", speed_hbm, speed_ref),
        ("left", left_hbm, left_ref),
        ("linv", linv_hbm, linv_ref),
        ("right", right_hbm, right_ref),
    ):
        loads[name] = pltpu.make_async_copy(source, target, load_sem.at[len(loads)])
        loads[name].start()

    def loaded(*names):
        for name in names:
            loads[name].wait()

    @pl.when(me_p == 0)
    def _():
        halo_in[0] = jnp.zeros(halo_in.shape[1:], f32)

    @pl.when(me_p == n_pen - 1)
    def _():
        halo_in[1] = jnp.zeros(halo_in.shape[1:], f32)

    barrier = pltpu.get_barrier_semaphore()

    def greet(where):
        pl.semaphore_signal(barrier, inc=1, device_id=where, device_id_type=MESH)
        return 0

    lax.fori_loop(1, n_blk, lambda off, _: greet({"blk": lax.rem(me_b + off, n_blk)}), 0)
    lax.fori_loop(1, n_pen, lambda off, _: greet({"pen": lax.rem(me_p + off, n_pen)}), 0)

    def met():
        pl.semaphore_wait(barrier, n_blk - 1 + n_pen - 1)

    lane = lax.broadcasted_iota(i32, (1, LANES), 1)
    lo_iota[...] = lax.broadcasted_iota(i32, (WIDE, LANES), 0).astype(f32).astype(jnp.bfloat16)

    def high_of(cells):
        wide = lax.shift_right_logical(cells, w_bits) & (wides - 1)
        return wide * depth + lax.shift_right_logical(cells, p_bits)

    def pick_lanes(cells):
        low = (cells & (WIDE - 1)).astype(f32).astype(jnp.bfloat16)
        return jnp.where(lo_iota[...] == low, jnp.bfloat16(1), jnp.bfloat16(0))

    loaded("owner")
    held = jnp.zeros((1, LANES), i32)
    for b in range(n_blk):
        held = jnp.where(lane == owner_ref[b], b, held)
    held_vec[...] = held
    held_copy = pltpu.make_async_copy(held_vec, held_ref, held_sem)
    held_copy.start()

    held_copy.wait()

    loaded("count", "state", "dcell", "dweight")
    tiles = [state_ref[m, :, w * WIDE : (w + 1) * WIDE] for m in range(nf) for w in range(wides)]
    n_rows = nf * n_hi
    parts[...] = jnp.concatenate(split(jnp.concatenate(tiles, axis=0)), axis=0)

    def fringe_offset(i):
        return n_blk // 2 + lax.div(i + 1, 2) * (2 * lax.rem(i, 2) - 1)

    def fringe_copy(slot, peer, source):
        return pltpu.make_async_remote_copy(
            src_ref=rows_out.at[slot],
            dst_ref=rows_in.at[source],
            send_sem=fringe_send.at[slot],
            recv_sem=fringe_recv.at[source],
            device_id={"blk": peer},
            device_id_type=MESH,
        )

    hi_iota = lax.broadcasted_iota(i32, (n_hi, LANES), 0)
    donors = dcell_ref.shape[1]

    across = lax.broadcasted_iota(i32, (LANES, WIDE), 1).astype(f32)

    def receivers(b):
        low = (rcell_ref[pl.ds(b, 1), :] & (WIDE - 1)).astype(f32)
        slots = jnp.broadcast_to(low, (LANES, LANES)).T
        slots = jnp.concatenate([slots] * (WIDE // LANES), axis=1)
        recv_lanes[b] = jnp.where(slots == across, 1.0, 0.0).astype(jnp.bfloat16)

    def send_ready(slot, _):
        fringe_copy(slot, lax.rem(me_b + fringe_offset(slot), n_blk), me_b).start()
        return 0

    together = min(TOGETHER, n_blk)
    steps = n_blk // together

    def interpolate(q, _):
        @pl.when(q == steps // 2)
        def _():
            met()
            lax.fori_loop(0, steps // 2 * together, send_ready, 0)

        for u in range(together):
            receivers(q * together + u)
        for u in range(together):
            slot = q * together + u
            peer = lax.rem(me_b + fringe_offset(slot), n_blk)
            block = held_ref[0, peer]
            cells, weights = dcell_ref[block], dweight_ref[block]
            acc = [None] * nf
            for i in range(0, donors, 2):
                pair = [cells[k : k + 1, :] for k in (i, i + 1)]
                picks = jnp.concatenate([pick_lanes(c) for c in pair], axis=1)
                both = jnp.dot(parts[...], picks, preferred_element_type=f32)
                both = both[:n_rows] + both[n_rows:]
                for k in range(2):
                    weight = jnp.where(hi_iota == high_of(pair[k]), weights[i + k : i + k + 1, :], 0.0)
                    for m in range(nf):
                        term = both[m * n_hi : (m + 1) * n_hi, k * LANES : (k + 1) * LANES] * weight
                        term = sum(term[w * depth : (w + 1) * depth] for w in range(wides))
                        acc[m] = term if acc[m] is None else acc[m] + term
            live = lane < count_ref[block]
            for m in range(nf):
                row = jnp.sum(acc[m], axis=0, keepdims=True)
                if m == 0:
                    row = jnp.where(live, row, DEAD)
                rows_out[slot, pl.ds(m, 1), :] = row

        @pl.when(q >= steps // 2)
        def _():
            for u in range(together - 1):
                send_ready(q * together + u, 0)

            @pl.when(q < steps - 1)
            def _():
                send_ready(q * together + together - 1, 0)

        return 0

    loaded("rcell")
    lax.fori_loop(0, steps, interpolate, 0)
    rows_in[me_b] = jnp.full(rows_in.shape[1:], DEAD, f32)

    placed[...] = jnp.zeros_like(placed)

    group = min(PLACED, n_blk)

    def place(q, _):
        sources = [lax.rem(me_b - fringe_offset(q * group + u) + n_blk, n_blk) for u in range(group)]
        for u in range(group - 1):
            fringe_copy(q * group + u, sources[u], sources[u]).wait_recv()
        last = q * group + group - 1

        @pl.when(last < n_blk - 1)
        def _():
            fringe_copy(last, sources[-1], sources[-1]).wait_recv()

        tall, flat = [], []
        for source in sources:
            block = held_ref[0, source]
            rows = [rows_in[source, m : m + 1, :] for m in range(nf)]
            here = (hi_iota == high_of(rcell_ref[pl.ds(block, 1), :])) & (rows[0] < 0.5 * DEAD)
            high, low = split(jnp.concatenate([jnp.where(here, row, 0.0) for row in rows], axis=0))
            hit = jnp.where(here, 1.0, 0.0).astype(jnp.bfloat16)
            tall.append(jnp.concatenate([high, low, hit], axis=0))
            flat.append(recv_lanes[block])
        placed[...] += jnp.dot(
            jnp.concatenate(tall, axis=1), jnp.concatenate(flat, axis=0), preferred_element_type=f32
        )
        return 0

    lax.fori_loop(0, n_blk // group, place, 0)
    for m in range(nf):
        for w in range(wides):
            at, lanes = m * n_hi + w * depth, slice(w * WIDE, (w + 1) * WIDE)
            value = placed[at : at + depth, :] + placed[n_rows + at : n_rows + at + depth, :]
            hit = placed[2 * n_rows + w * depth : 2 * n_rows + (w + 1) * depth, :]
            filled[m, :, lanes] = jnp.where(hit > 0.5, value, state_ref[m, :, lanes])

    def halo_copy(way, peer):
        return pltpu.make_async_remote_copy(
            src_ref=halo_out.at[way],
            dst_ref=halo_in.at[way],
            send_sem=halo_send.at[way],
            recv_sem=halo_recv.at[way],
            device_id={"pen": peer},
            device_id_type=MESH,
        )

    halo_out[0] = filled[:, depth - 2 :, :]
    halo_out[1] = filled[:, :2, :]
    upward = halo_copy(0, lax.rem(me_p + 1, n_pen))
    downward = halo_copy(1, lax.rem(me_p + n_pen - 1, n_pen))

    @pl.when(me_p < n_pen - 1)
    def _():
        upward.start()

    @pl.when(me_p > 0)
    def _():
        downward.start()

    loaded("prev", "iblank", "speed", "left")
    layer = lax.broadcasted_iota(i32, (depth, pencils), 0)
    keep = iblank_ref[...].astype(f32)

    def wave(m):
        return jnp.concatenate([speed_ref[m * groups + g : m * groups + g + 1, :] for g in range(groups)], axis=1)

    for m in range(nf):
        cur = filled[m]
        upper = jnp.where(layer == depth - 1, 0.0, pltpu.roll(cur, depth - 1, 0))
        upper_two = jnp.where(layer >= depth - 2, 0.0, pltpu.roll(cur, depth - 2, 0))
        lower = jnp.where(layer == 0, 0.0, pltpu.roll(cur, 1, 0))
        lower_two = jnp.where(layer <= 1, 0.0, pltpu.roll(cur, 2, 0))
        r = -(cur - prev_ref[m]) - 0.5 * wave(m) * (upper - lower)
        r = r + 0.25 * (upper - 2.0 * cur + lower)
        r = r - 0.0625 * (upper_two - 4.0 * upper + 6.0 * cur - 4.0 * lower + lower_two)
        r = r - 0.25 * (pltpu.roll(cur, pencils - 1, 1) - pltpu.roll(cur, 1, 1))
        resid[m] = r * keep

    def mix(matrix_ref, value, m, g):
        total = None
        for n in range(nf):
            at = (m * nf + n) * groups + g
            term = matrix_ref[at : at + 1, :] * value(n, g)
            total = term if total is None else total + term
        return total

    def resid_at(n, g):
        return resid[n, :, g * LANES : (g + 1) * LANES]

    def place_of(m, g):
        return (g % 2, g, 2) if m == 4 else (m // 2, g, m % 2)

    def each_peer(do):
        lax.fori_loop(0, n_a, lambda i, _: do(1 - zh, lax.rem(a + i, n_a)), 0)
        lax.fori_loop(1, n_a, lambda i, _: do(zh, lax.rem(a + i, n_a)), 0)

    def each_source(do):
        lax.fori_loop(1, n_a, lambda i, _: do(zh, lax.rem(a + n_a - i, n_a)), 0)
        lax.fori_loop(0, n_a, lambda i, _: do(1 - zh, lax.rem(a + n_a - i, n_a)), 0)

    def takes_third(half, g):
        return lax.rem(g, 2) == half

    MESSAGES = ((0, 0, 2), (1, 0, 2))
    ANSWERS = ((0, 2),)

    def sized(first, count, more, do):
        if first + count < 2:
            do(count)
            return 0

        @pl.when(more)
        def _():
            do(count + 1)

        @pl.when(jnp.logical_not(more))
        def _():
            do(count)

        return 0

    def fwd_copy(message, half, g, source, count):
        part, first, _ = MESSAGES[message]
        peer = half * n_a + g
        return pltpu.make_async_remote_copy(
            src_ref=work.at[part, half, g, pl.ds(first, count)],
            dst_ref=parts_in.at[part, source, pl.ds(first, count)],
            send_sem=fwd_send.at[message, peer],
            recv_sem=fwd_recv.at[message, source],
            device_id={"pen": peer},
            device_id_type=MESH,
        )

    def send_message(message):
        part, first, count = MESSAGES[message]
        each_peer(
            lambda half, g: sized(
                first, count, takes_third(half, g), lambda n: fwd_copy(message, half, g, me_p, n).start()
            )
        )

        def keep_own(n):
            parts_in[part, me_p, first : first + n] = work[part, zh, a, first : first + n]

        sized(first, count, third, keep_own)

    for g in range(groups):
        for m in range(nf):
            work[(0, *place_of(m, g))] = mix(left_ref, resid_at, m, g)[2 : depth - 2, :]
    send_message(0)

    @pl.when(me_p > 0)
    def _():
        upward.wait_recv()

    @pl.when(me_p < n_pen - 1)
    def _():
        downward.wait_recv()

    for m in range(nf):
        low2, low1 = halo_in[0, m, 0:1, :], halo_in[0, m, 1:2, :]
        up1, up2 = halo_in[1, m, 0:1, :], halo_in[1, m, 1:2, :]
        speed = wave(m)
        first = (0.5 + 0.5 * speed) * low1 - 0.0625 * low2
        last = (0.5 - 0.5 * speed) * up1 - 0.0625 * up2
        second, last_but = -0.0625 * low1, -0.0625 * up1
        extra = jnp.where(
            layer == 0,
            first,
            jnp.where(layer == 1, second, jnp.where(layer == depth - 1, last, jnp.where(layer == depth - 2, last_but, 0.0))),
        )
        resid[m] = resid[m] + extra * keep

    for g in range(groups):
        for m in range(nf):
            half, at, f = place_of(m, g)
            mixed = mix(left_ref, resid_at, m, g)
            work[1, half, at, f, 0:2, :] = mixed[0:2, :]
            work[1, half, at, f, 2:4, :] = mixed[depth - 2 :, :]
    send_message(1)

    def fringe_left(i, _):
        fringe_copy(i, me_b, me_b).wait_send()
        return 0

    lax.fori_loop(0, n_blk - 1, fringe_left, 0)

    @pl.when(me_p < n_pen - 1)
    def _():
        upward.wait_send()

    @pl.when(me_p > 0)
    def _():
        downward.wait_send()

    loaded("linv", "right")
    def await_message(message):
        _, first, count = MESSAGES[message]
        each_source(
            lambda half, g: sized(
                first, count, third, lambda n: fwd_copy(message, half, g, half * n_a + g, n).wait_recv()
            )
        )

    def solve(f):
        for p in range(n_pen):
            work_line[p * depth : p * depth + 2, :] = parts_in[1, p, f, 0:2, :]
            work_line[p * depth + 2 : p * depth + 6, :] = parts_in[0, p, f]
            work_line[p * depth + 6 : (p + 1) * depth, :] = parts_in[1, p, f, 2:4, :]
        inv_high, inv_low = split(linv_ref[4 if f == 2 else zh * 2 + f])
        line_high, line_low = split(work_line[...])
        line = jnp.dot(
            jnp.concatenate([inv_high, inv_high, inv_low], axis=1),
            jnp.concatenate([line_high, line_low, line_high], axis=0),
            preferred_element_type=f32,
        )
        for p in range(n_pen):
            solved_line[p, f] = line[p * depth : (p + 1) * depth, :]

    def back_copy(answer, peer, half, g, count):
        first = ANSWERS[answer][0]
        return pltpu.make_async_remote_copy(
            src_ref=solved_line.at[peer, pl.ds(first, count)],
            dst_ref=solved.at[half, g, pl.ds(first, count)],
            send_sem=back_send.at[answer, peer],
            recv_sem=back_recv.at[answer, half * n_a + g],
            device_id={"pen": peer},
            device_id_type=MESH,
        )

    def send_answer(answer):
        first, count = ANSWERS[answer]
        each_peer(
            lambda half, g: sized(
                first, count, third, lambda n: back_copy(answer, half * n_a + g, zh, a, n).start()
            )
        )

        def keep_solved(n):
            solved[zh, a, first : first + n] = solved_line[me_p, first : first + n]

        sized(first, count, third, keep_solved)

    await_message(0)
    await_message(1)
    solve(0)
    solve(1)

    @pl.when(third)
    def _():
        solve(2)

    send_answer(0)

    def left(half, g):
        for message, (_, first, count) in enumerate(MESSAGES):
            sized(first, count, takes_third(half, g), lambda n: fwd_copy(message, half, g, me_p, n).wait_send())
        for answer, (first, count) in enumerate(ANSWERS):
            sized(first, count, third, lambda n: back_copy(answer, half * n_a + g, zh, a, n).wait_send())
        return 0

    each_peer(left)

    def answered(half, g):
        for answer, (first, count) in enumerate(ANSWERS):
            sized(
                first, count, takes_third(half, g), lambda n: back_copy(answer, half * n_a + g, half, g, n).wait_recv()
            )
        return 0

    each_source(answered)

    def solved_at(n, g):
        return solved[place_of(n, g)]

    for g in range(groups):
        lanes = slice(g * LANES, (g + 1) * LANES)
        for m in range(nf):
            out_ref[m, :, lanes] = filled[m, :, lanes] + keep[:, lanes] * mix(right_ref, solved_at, m, g)


def solution(mesh):
    n_blk, n_pen = mesh.shape["blk"], mesh.shape["pen"]

    def shards(
        state,
        previous,
        iblank,
        block_owner,
        donor_cell,
        donor_weight,
        send_count,
        recv_cell,
        speed,
        left_vectors,
        right_vectors,
        line_inverse,
    ):
        _, depth, nf, pencils = state.shape
        groups, n_hi = pencils // LANES, pencils // WIDE * depth
        points = line_inverse.shape[-1]
        cap, donors = recv_cell.shape[-1], donor_cell.shape[-1]
        f32 = jnp.float32
        hbm = pl.BlockSpec(memory_space=pltpu.HBM)
        vmem = pl.BlockSpec(memory_space=pltpu.VMEM)
        dma = pltpu.SemaphoreType.DMA
        out = pl.pallas_call(
            functools.partial(kernel, n_blk, n_pen),
            out_shape=jax.ShapeDtypeStruct((nf, depth, pencils), f32),
            in_specs=[hbm] * 12,
            out_specs=vmem,
            scratch_shapes=[
                pltpu.SMEM((n_blk,), jnp.int32),
                pltpu.SMEM((n_blk,), jnp.int32),
                pltpu.VMEM((nf, depth, pencils), f32),
                pltpu.VMEM((nf, depth, pencils), f32),
                pltpu.VMEM((depth, pencils), jnp.int32),
                pltpu.VMEM((n_blk, donors, cap), jnp.int32),
                pltpu.VMEM((n_blk, donors, cap), f32),
                pltpu.VMEM((n_blk, cap), jnp.int32),
                pltpu.VMEM((nf * groups, LANES), f32),
                pltpu.VMEM((nf * nf * groups, LANES), f32),
                pltpu.VMEM((nf * nf * groups, LANES), f32),
                pltpu.VMEM((nf, points, points), f32),
                dma((12,)),
                pltpu.VMEM((1, LANES), jnp.int32),
                pltpu.SMEM((1, LANES), jnp.int32),
                dma(()),
                pltpu.VMEM((WIDE, LANES), jnp.bfloat16),
                pltpu.VMEM((n_blk, LANES, WIDE), jnp.bfloat16),
                pltpu.VMEM((2 * nf * n_hi, WIDE), jnp.bfloat16),
                pltpu.VMEM(((2 * nf + 1) * n_hi, WIDE), f32),
                pltpu.VMEM((n_blk, nf, cap), f32),
                pltpu.VMEM((n_blk, nf, cap), f32),
                pltpu.VMEM((nf, depth, pencils), f32),
                pltpu.VMEM((2, nf, 2, pencils), f32),
                pltpu.VMEM((2, nf, 2, pencils), f32),
                pltpu.VMEM((nf, depth, pencils), f32),
                pltpu.VMEM((2, 2, groups, 3, depth // 2, LANES), f32),
                pltpu.VMEM((2, n_pen, 3, depth // 2, LANES), f32),
                pltpu.VMEM((points, LANES), f32),
                pltpu.VMEM((n_pen, 3, depth, LANES), f32),
                pltpu.VMEM((2, groups, 3, depth, LANES), f32),
                dma((n_blk,)),
                dma((n_blk,)),
                dma((2,)),
                dma((2,)),
                dma((2, n_pen)),
                dma((2, n_pen)),
                dma((1, n_pen)),
                dma((1, n_pen)),
            ],
            compiler_params=pltpu.CompilerParams(
                collective_id=0, has_side_effects=True, vmem_limit_bytes=60 * 1024 * 1024
            ),
        )(
            block_owner,
            send_count.reshape(n_blk),
            state[0].transpose(1, 0, 2),
            previous[0].transpose(1, 0, 2),
            iblank[0],
            donor_cell[0, 0].transpose(0, 2, 1),
            donor_weight[0, 0].transpose(0, 2, 1),
            recv_cell[0, 0],
            speed.reshape(nf * groups, LANES),
            left_vectors.reshape(nf * nf * groups, LANES),
            right_vectors.reshape(nf * nf * groups, LANES),
            line_inverse[0],
        )
        return out.transpose(1, 0, 2)[None]

    placed = (
        P("blk", "pen", None, None),
        P("blk", "pen", None, None),
        P("blk", "pen", None),
        P(),
        P("pen", "blk", None, None, None),
        P("pen", "blk", None, None, None),
        P("pen", "blk", None),
        P("pen", "blk", None, None),
        P("blk", None, None),
        P("blk", None, None, None),
        P("blk", None, None, None),
        P("blk", None, None, None),
    )
    return jax.shard_map(
        shards, mesh=mesh, in_specs=placed, out_specs=P("blk", "pen", None, None), check_vma=False
    )
```
